32 devices in a mesh: cpi: 2 (over x), elem: 16 (over z, y, core).
Axes of the slice: x: 2, y: 2, z: 4, core: 2. Of those that a mesh axis runs over, the one named last changes fastest.
Arguments:
- raw_echo: bfloat16 [256, 2, 128, 3072], P(('cpi', 'elem')), parts along dimension 0, may hold values from -6 to 6
- beam_weights: bfloat16 [8, 2, 128], replicated, may hold values from -0.375 to 0.375
- steer: float32 [2, 24], replicated, may hold values from -4 to 4
- train_mask: int32 [256, 3072], P(('cpi', 'elem')), parts along dimension 0, may hold values 0 or 1
Outputs:
- filtered: float32 [256, 2, 3072], P(('cpi', 'elem')), parts along dimension 0
The draws below stay inside these ranges and needn't reach their ends.
There are 2 independent parts, one for each index of `cpi`. The reference program is written for one: setup_inputs(seed, part) draws one part's arguments, and reference() takes and returns one part's arrays. A program takes and returns all parts, laid end to end along the dimension named above; an argument that names none is the same for every part. Nothing has to cross between parts.
All inputs are finite; a program needn't handle non-finite values. No bound on the sum of `train_mask` on one device may be relied on, other than what follows from the above.
Results may differ from the reference program's by a relative error of at most 0.0044.
Values may be sent and summed in bfloat16 or wider, within the bound.
No kernel may reach another device: no remote copies, remote signals or barrier semaphores. Data moves between devices by JAX's collectives and lax.ppermute only.
A program may use at most 128 MiB of HBM per device.

```python
import math
import jax
import jax.numpy as jnp
from jax import lax

ELEM_DEV = 8
BEAMS = 8
PULSES = 128
GATES = 3072
ELEMENTS = 128
N_ELEM = 16


def touch_ends(drawn, own_key, least, top_value):
    spot = [jax.random.randint(jax.random.fold_in(own_key, axis), (), 0, length) for axis, length in enumerate(drawn.shape)]
    main_axis = drawn.shape.index(max(drawn.shape))
    neighbour = spot[:main_axis] + [(spot[main_axis] + 1) % drawn.shape[main_axis]] + spot[main_axis + 1:]
    return drawn.at[tuple(spot)].set(least).at[tuple(neighbour)].set(top_value)


def level_of(stream_key, dims, cuts, least, high):
    factor_of = 1.0
    for dim, parts in cuts:
        steps = jax.random.uniform(jax.random.fold_in(jax.random.fold_in(stream_key, 6), dim), (parts,), jnp.float32, least / len(cuts), high / len(cuts))
        factor_of = factor_of * jnp.repeat(jnp.exp(steps), dims[dim] // parts).reshape((-1,) + (1,) * (len(dims) - 1 - dim))
    return factor_of


def normal_values(stream_key, extent, scale, limit, shards=(), held_as=jnp.bfloat16):
    loudness = level_of(stream_key, extent, shards, -0.22, 0.18) if shards else 1.0
    drawn = jax.random.normal(stream_key, extent, jnp.float32) * scale * loudness
    return jnp.minimum(jnp.maximum(drawn, -limit), limit).astype(held_as)


def setup_inputs(seed: int = 0, part: int = 0) -> dict:
    keys = jax.random.split(jax.random.key(seed), 5)
    own_keys = jax.random.split(jax.random.fold_in(keys[4], part), 5)
    return {
        "raw_echo": normal_values(own_keys[0], (ELEMENTS, 2, PULSES, GATES), 1.0, 6.0, ((0, 16),)),
        "beam_weights": normal_values(keys[1], (BEAMS, 2, ELEMENTS), (2 * ELEMENTS) ** -0.5, 0.375),
        "steer": normal_values(keys[2], (2, 3 * BEAMS), 0.3, 4.0, (), jnp.float32),
        "train_mask": touch_ends((jax.random.randint(own_keys[3], (PULSES, GATES), 0, 4) < 1).astype(jnp.int32), jax.random.fold_in(own_keys[3], 1), 0, 1),
    }


LOADING = 1.0

def doppler_table(pulses):
    doppler_index = jnp.arange(pulses, dtype=jnp.int32)
    phase = doppler_index[:, None] * doppler_index[None, :] % pulses
    angles = -2.0 * math.pi / pulses * phase.astype(jnp.float32)
    cosine = jnp.cos(angles) / math.sqrt(pulses)
    sine_part = jnp.sin(angles) / math.sqrt(pulses)
    real_row = jnp.concatenate([cosine, -sine_part], axis=1)
    imag_row = jnp.concatenate([sine_part, cosine], axis=1)
    return jnp.stack([real_row, imag_row], axis=1).astype(jnp.bfloat16)

def beam_matrix(beam_weights):
    beam_count = beam_weights.shape[0]
    elem_count = beam_weights.shape[2]
    weight_re = beam_weights[:, 0, :]
    weight_im = beam_weights[:, 1, :]
    real_row = jnp.stack([weight_re, -weight_im], axis=2).reshape(beam_count, 2 * elem_count)
    imag_row = jnp.stack([weight_im, weight_re], axis=2).reshape(beam_count, 2 * elem_count)
    return jnp.concatenate([real_row, imag_row], axis=0)

def adapt(window, train_mask, steer):
    bins_here = window.shape[0]
    gate_count = window.shape[-1]
    beam_count = window.shape[2] // 2
    stacked = window.reshape(bins_here, 3, 2, beam_count, gate_count).transpose(0, 2, 1, 3, 4)
    stacked = stacked.reshape(bins_here, 6 * beam_count, gate_count)
    picked = stacked * train_mask[:, None, :].astype(jnp.float32)
    gram_sums = jnp.einsum('nig,njg->nij', picked, stacked, precision=lax.Precision.HIGHEST)
    half_dim = 3 * beam_count
    upper_left = gram_sums[:, :half_dim, :half_dim]
    upper_right = gram_sums[:, :half_dim, half_dim:]
    lower_left = gram_sums[:, half_dim:, :half_dim]
    lower_right = gram_sums[:, half_dim:, half_dim:]
    identity = jnp.eye(half_dim, dtype=jnp.float32)
    real_part = upper_left + lower_right + LOADING * identity[None]
    imag_part = lower_left - upper_right
    system = jnp.concatenate([jnp.concatenate([real_part, -imag_part], axis=2), jnp.concatenate([imag_part, real_part], axis=2)], axis=1)
    target = steer.reshape(-1)
    factor = jnp.linalg.cholesky(system)
    solved = jax.vmap(lambda factor_one: jax.scipy.linalg.cho_solve((factor_one, True), target))(factor)
    response = lax.optimization_barrier(jnp.sum(solved * target[None, :], axis=1))
    weight = solved / response[:, None]
    weight_re = weight[:, :half_dim]
    weight_im = weight[:, half_dim:]
    snap_re = stacked[:, :half_dim]
    snap_im = stacked[:, half_dim:]
    highest = lax.Precision.HIGHEST
    output_re = jnp.einsum('ni,nig->ng', weight_re, snap_re, precision=highest) + jnp.einsum('ni,nig->ng', weight_im, snap_im, precision=highest)
    output_im = jnp.einsum('ni,nig->ng', weight_re, snap_im, precision=highest) - jnp.einsum('ni,nig->ng', weight_im, snap_re, precision=highest)
    return jnp.stack([output_re, output_im], axis=1)

def reference(raw_echo, beam_weights, steer, train_mask):
    pulses = raw_echo.shape[2]
    gate_count = raw_echo.shape[3]
    dft_table = doppler_table(pulses)
    matrix = beam_matrix(beam_weights)
    rows_out = matrix.shape[0]
    echo_blocks = raw_echo.reshape(N_ELEM, ELEM_DEV, 2 * pulses, gate_count)
    column_blocks = matrix.reshape(rows_out, N_ELEM, 2 * ELEM_DEV).transpose(1, 0, 2)

    def accumulate(total, pieces):
        echo_block, column_block = pieces
        spectra_rows = jnp.einsum('dcr,erg->decg', dft_table.astype(jnp.float32), echo_block.astype(jnp.float32), preferred_element_type=jnp.float32).astype(jnp.bfloat16)
        spectra_rows = spectra_rows.reshape(pulses, 2 * ELEM_DEV, gate_count)
        return (total + jnp.einsum('ok,dkg->dog', column_block.astype(jnp.float32), spectra_rows.astype(jnp.float32), preferred_element_type=jnp.float32), None)
    beam_rows, unused = lax.scan(accumulate, jnp.zeros((pulses, rows_out, gate_count), jnp.float32), (echo_blocks, column_blocks))
    window = jnp.stack([jnp.roll(beam_rows, 1, 0), beam_rows, jnp.roll(beam_rows, -1, 0)], axis=1)
    return adapt(window, train_mask, steer)
```

```python
import functools
import math

import jax
import jax.numpy as jnp
import numpy as np
from jax import lax
from jax.experimental import pallas as pl
from jax.experimental.pallas import tpu as pltpu
from jax.sharding import PartitionSpec as P

LOADING = 1.0
F32 = jnp.float32
BF16 = jnp.bfloat16
GROUP = 16
CHUNKS = ((3, 0), (6, 0), (6, 0), (6, 0), (3, 0))


def bin_order(strides):
    count = len(strides)
    blocks = []
    for position in range(1 << count):
        blocks.append(sum(s for i, s in enumerate(strides) if position >> (count - 1 - i) & 1))
    return np.array(blocks, np.int32)


def doppler_table(me, strides, bins_here, pulses):
    owners = jnp.bitwise_xor(me, jnp.asarray(bin_order(strides)))
    bins = (owners[:, None] * bins_here + jnp.arange(bins_here, dtype=jnp.int32)).reshape(-1)
    phase = bins[:, None] * jnp.arange(pulses, dtype=jnp.int32)[None, :] % pulses
    angles = -2.0 * math.pi / pulses * phase.astype(F32)
    cosine = jnp.cos(angles) / math.sqrt(pulses)
    sine_part = jnp.sin(angles) / math.sqrt(pulses)
    real_row = jnp.concatenate([cosine, -sine_part], axis=1)
    imag_row = jnp.concatenate([sine_part, cosine], axis=1)
    return jnp.stack([real_row, imag_row], axis=1).astype(BF16).reshape(2 * pulses, 2 * pulses)


def block_weights(beam_weights, me, elem_dev):
    mine = lax.dynamic_slice_in_dim(beam_weights, me * elem_dev, elem_dev, 2)
    weight_re, weight_im = mine[:, 0, :], mine[:, 1, :]
    real_row = jnp.stack([weight_re, -weight_im], axis=2)
    imag_row = jnp.stack([weight_im, weight_re], axis=2)
    matrix = jnp.concatenate([real_row, imag_row], axis=0)
    same = jnp.eye(GROUP, dtype=BF16)
    full = same[:, None, None, :, None] * matrix[None, :, :, None, :]
    return full.reshape(GROUP * matrix.shape[0], elem_dev * GROUP * 2)


def front_kernel(table_ref, weights_ref, echo_ref, send_ref, keep_ref, spectra_ref):
    elem_dev = echo_ref.shape[0]
    groups = spectra_ref.shape[0]
    width = echo_ref.shape[-1]
    table = table_ref[...]
    for e in range(elem_dev):
        spectra = jnp.dot(table, echo_ref[e], preferred_element_type=F32)
        spectra_ref[:, e] = spectra.astype(BF16).reshape(groups, 2 * GROUP, width)
    weights = weights_ref[...]
    rows = weights.shape[0]
    for g in range(groups):
        beams = jnp.dot(weights, spectra_ref[g].reshape(-1, width), preferred_element_type=F32)
        at = g % (groups // 2) * rows
        if g < groups // 2:
            keep_ref[at : at + rows] = beams
        else:
            send_ref[at : at + rows] = beams.astype(BF16)


def front(table, weights, echo, start, size, width):
    elem_dev, rows_in, _ = echo.shape
    groups = rows_in // 2 // GROUP
    half = rows_in // 4 * (weights.shape[0] // GROUP)
    steps = size // width
    first = start // width
    return pl.pallas_call(
        front_kernel,
        grid=(steps,),
        in_specs=[
            pl.BlockSpec(table.shape, lambda i: (0, 0)),
            pl.BlockSpec(weights.shape, lambda i: (0, 0)),
            pl.BlockSpec((elem_dev, rows_in, width), lambda i: (0, 0, first + i)),
        ],
        out_specs=[
            pl.BlockSpec((half, width), lambda i: (0, i)),
            pl.BlockSpec((half, width), lambda i: (0, i)),
        ],
        out_shape=[
            jax.ShapeDtypeStruct((half, size), BF16),
            jax.ShapeDtypeStruct((half, size), F32),
        ],
        scratch_shapes=[pltpu.VMEM((groups, elem_dev, 2 * GROUP, width), BF16)],
        compiler_params=pltpu.CompilerParams(vmem_limit_bytes=48 << 20),
        cost_estimate=pl.CostEstimate(
            flops=4 * elem_dev * rows_in * rows_in * size,
            bytes_accessed=elem_dev * rows_in * size * 2 + half * size * 6,
            transcendentals=0,
        ),
        name="front",
    )(table, weights, echo)


def gram_kernel(own_ref, low_ref, high_ref, mask_ref, gram_ref):
    bins_here = mask_ref.shape[0]
    rows = low_ref.shape[0]
    window = jnp.concatenate([low_ref[...], own_ref[...], high_ref[...]], axis=0)
    top = window.astype(BF16)
    rest = (window - top.astype(F32)).astype(BF16)
    mask = mask_ref[...].astype(F32)
    picked_top, picked_rest = [], []
    for d in range(bins_here):
        keep = mask[d : d + 1].astype(BF16)
        picked_top.append(top[rows * d : rows * (d + 3)] * keep)
        picked_rest.append(rest[rows * d : rows * (d + 3)] * keep)
    left = jnp.concatenate(picked_top, axis=0)
    left_rest = jnp.concatenate(picked_rest, axis=0)
    dims = (((1,), (1,)), ((), ()))
    gram = lax.dot_general(left, top, dims, preferred_element_type=F32)
    gram += lax.dot_general(left, rest, dims, preferred_element_type=F32)
    gram += lax.dot_general(left_rest, top, dims, preferred_element_type=F32)
    gram_ref[...] = gram


def gram_of(own, low, high, mask):
    bins_here, size = mask.shape
    rows = low.shape[0]
    return pl.pallas_call(
        gram_kernel,
        out_shape=jax.ShapeDtypeStruct((bins_here * 3 * rows, (bins_here + 2) * rows), F32),
        compiler_params=pltpu.CompilerParams(vmem_limit_bytes=48 << 20),
        cost_estimate=pl.CostEstimate(
            flops=6 * bins_here * 3 * rows * (bins_here + 2) * rows * size,
            bytes_accessed=(bins_here + 2) * rows * size * 4,
            transcendentals=0,
        ),
        name="gram",
    )(own, low, high, mask)


def tail_kernel(count, *refs):
    steer_ref, refs = refs[0], refs[1:]
    grams, refs = refs[:count], refs[count:]
    owns, lows, highs = refs[:count], refs[count : 2 * count], refs[2 * count : 3 * count]
    out_ref = refs[3 * count]
    window_ref = refs[3 * count + 1]
    rows = lows[0].shape[0]
    beams = rows // 2
    bins_here = owns[0].shape[0] // rows
    order = 3 * beams
    at = 0
    spans = []
    for own, low, high in zip(owns, lows, highs):
        size = own.shape[1]
        spans.append((at, size))
        at += size
    gram = grams[0][...]
    for other in grams[1:]:
        gram += other[...]

    lane = lax.broadcasted_iota(jnp.int32, (1, 1, 128), 2)
    real_lane = lane // beams % 2 == 0
    row_at = lax.broadcasted_iota(jnp.int32, (1, order, 128), 1)
    lane_at = lax.broadcasted_iota(jnp.int32, (1, order, 128), 2)
    column_of = lane_at // rows * beams + lane_at % beams
    diagonal = (column_of == row_at) & (lane_at // beams % 2 == 0) & (lane_at < 3 * rows)
    systems = []
    pad = jnp.zeros((3 * rows, 128 - 3 * rows), F32)
    for d in range(bins_here):
        block = gram[3 * rows * d : 3 * rows * (d + 1), rows * d : rows * (d + 3)]
        block = jnp.concatenate([block, pad], axis=1)
        from_re = jnp.concatenate([block[rows * w : rows * w + beams] for w in range(3)], axis=0)
        from_im = jnp.concatenate(
            [block[rows * w + beams : rows * (w + 1)] for w in range(3)], axis=0
        )
        real = from_re + pltpu.roll(from_im, 128 - beams, 1)
        imag = pltpu.roll(from_im, beams, 1) - from_re
        systems.append(jnp.where(real_lane[0], real, imag))
    steer = steer_ref[...]
    system = jnp.stack(systems, axis=0)
    system = jnp.where(lane < 3 * rows, system, 0.0) + jnp.where(diagonal, LOADING, 0.0)
    system = system + steer[None]

    def swapped(row):
        return jnp.where(
            real_lane, -pltpu.roll(row, 128 - beams, 2), pltpu.roll(row, beams, 2)
        )

    for k in range(order):
        spot = k // beams * rows + k % beams
        pivot_row = system[:, k : k + 1, :]
        pivot_row = pivot_row / pivot_row[:, :, spot : spot + 1]
        factor_re = system[:, :, spot : spot + 1]
        factor_im = system[:, :, spot + beams : spot + beams + 1]
        changed = system - factor_re * pivot_row - factor_im * swapped(pivot_row)
        system = jnp.where(row_at == k, pivot_row, changed)

    solved_re = system[:, :, 3 * rows : 3 * rows + 1]
    solved_im = system[:, :, 3 * rows + beams : 3 * rows + beams + 1]
    target_re = steer[None, :, 3 * rows : 3 * rows + 1]
    target_im = steer[None, :, 3 * rows + beams : 3 * rows + beams + 1]
    response = jnp.sum(solved_re * target_re + solved_im * target_im, axis=1, keepdims=True)
    weight_re = jnp.broadcast_to(solved_re / response, (bins_here, order, 128))
    weight_im = jnp.broadcast_to(solved_im / response, (bins_here, order, 128))

    for index, (start, size) in enumerate(spans):
        for low_lane in range(0, size, 128):
            lanes = slice(low_lane, low_lane + 128)
            blocks = []
            for ref in (lows[index], owns[index], highs[index]):
                part = ref[:, lanes]
                blocks += [part[i : i + beams] for i in range(0, part.shape[0], beams)]
            for d in range(bins_here):
                total_re = jnp.zeros((beams, 128), F32)
                total_im = jnp.zeros((beams, 128), F32)
                for w in range(3):
                    coeff_re = weight_re[d, w * beams : (w + 1) * beams]
                    coeff_im = weight_im[d, w * beams : (w + 1) * beams]
                    snap_re, snap_im = blocks[2 * (d + w)], blocks[2 * (d + w) + 1]
                    total_re += coeff_re * snap_re + coeff_im * snap_im
                    total_im += coeff_re * snap_im - coeff_im * snap_re
                both = jnp.concatenate(
                    [
                        jnp.sum(total_re, axis=0, keepdims=True),
                        jnp.sum(total_im, axis=0, keepdims=True),
                    ],
                    axis=0,
                )
                out_ref[d, :, start + low_lane : start + low_lane + 128] = both


def tail(steer, grams, owns, lows, highs, bins_here):
    gate_count = sum(own.shape[1] for own in owns)
    count = len(owns)
    rows = lows[0].shape[0]
    return pl.pallas_call(
        functools.partial(tail_kernel, count),
        out_shape=jax.ShapeDtypeStruct((bins_here, 2, gate_count), F32),
        scratch_shapes=[pltpu.VMEM((8, 128), F32)],
        compiler_params=pltpu.CompilerParams(vmem_limit_bytes=48 << 20),
        name="tail",
    )(steer, *grams, *owns, *lows, *highs)


def steer_lanes(steer, beams):
    order = steer.shape[1]
    rows = 2 * beams
    return jnp.concatenate(
        [
            jnp.zeros((order, 3 * rows), F32),
            steer[0][:, None],
            jnp.zeros((order, beams - 1), F32),
            steer[1][:, None],
            jnp.zeros((order, 128 - 3 * rows - beams - 1), F32),
        ],
        axis=1,
    )


def swap(x, stride, count):
    return lax.ppermute(x, "elem", [(i, i ^ stride) for i in range(count)])


def reduce_chunk(send, keep, strides, count):
    received = [swap(send, strides[0], count)]
    size = keep.shape[0]
    for stride in strides[1:]:
        size //= 2
        total = keep[size : 2 * size]
        for got in received:
            total = total + got[size : 2 * size].astype(F32)
        received.append(swap(total.astype(BF16), stride, count))
    total = keep[:size]
    for got in received:
        total = total + got[:size].astype(F32)
    return total


def local(raw_echo, beam_weights, steer, train_mask):
    elem_dev, _, pulses, gate_count = raw_echo.shape
    count = lax.axis_size("elem")
    me = lax.axis_index("elem")
    bins_here = pulses // count
    beams = beam_weights.shape[0]
    rows = 2 * beams
    echo = raw_echo.reshape(elem_dev, 2 * pulses, gate_count)
    weights = block_weights(beam_weights, me, elem_dev)
    levels = count.bit_length() - 1
    plain = [1 << i for i in range(levels)]
    other = [plain[0], plain[2], plain[1]] + plain[3:]
    orders = [plain, other]
    tables = {
        kind: doppler_table(me, orders[kind], bins_here, pulses)
        for kind in sorted({kind for _, kind in CHUNKS})
    }
    unit = gate_count // sum(width for width, _ in CHUNKS)
    start = 0
    owns, lows, highs, grams = [], [], [], []
    up = [(i, (i + 1) % count) for i in range(count)]
    down = [((i + 1) % count, i) for i in range(count)]
    for width, kind in CHUNKS:
        size = width * unit
        send, keep = front(tables[kind], weights, echo, start, size, 3 * unit)
        own = reduce_chunk(send, keep, orders[kind], count)
        low = lax.ppermute(own[-rows:], "elem", up)
        high = lax.ppermute(own[:rows], "elem", down)
        grams.append(gram_of(own, low, high, train_mask[:, start : start + size]))
        owns.append(own)
        lows.append(low)
        highs.append(high)
        start += size
    return tail(steer_lanes(steer, beams), grams, owns, lows, highs, bins_here)


def solution(mesh):
    return jax.shard_map(
        local,
        mesh=mesh,
        in_specs=(P(("cpi", "elem"), None, None, None), P(), P(), P(("cpi", "elem"), None)),
        out_specs=P(("cpi", "elem"), None, None),
        check_vma=False,
    )
```

```python
import functools
import math

import jax
import jax.numpy as jnp
import ml_dtypes
import numpy as np
from jax import lax
from jax.experimental import pallas as pl
from jax.experimental.pallas import tpu as pltpu
from jax.sharding import PartitionSpec as P

LOADING = 1.0
F32 = jnp.float32
BF16 = jnp.bfloat16
GROUP = 8
VMEM = 48 << 20
CHUNKS = ((2, 0, 0), (2, 1, 0), (3, 0, 0), (3, 0, 0), (2, 0, 1))
STEPS = (
    (0, 0), (1, 0), (0, 1), (2, 0), (1, 1), (3, 0), (2, 1), (0, 2), (1, 2), (4, 0), (3, 1), (0, 3), (2, 2), (1, 3),
    (0, 4), (4, 1), (2, 3), (3, 2), (1, 4), (2, 4), (3, 3), (4, 2), (4, 3), (3, 4), ("halo", 0), ("gram", 0), (4, 4),
)


def block_at(strides):
    count = len(strides)
    blocks = []
    for position in range(1 << count):
        blocks.append(sum(s for i, s in enumerate(strides) if position >> (count - 1 - i) & 1))
    return blocks


def row_order(strides, bins_here, extra):
    rows = []
    for block in block_at(strides):
        for j in range(-extra, bins_here + extra):
            rows += [(block, 2 * j), (block, 2 * j + 1)]
    return np.array(rows, np.int32)


def doppler_table(pulses):
    index = np.arange(pulses)
    angles = (-2.0 * math.pi / pulses * (index[:, None] * index[None, :] % pulses)).astype(np.float32)
    cosine = np.cos(angles) / np.float32(math.sqrt(pulses))
    sine_part = np.sin(angles) / np.float32(math.sqrt(pulses))
    real_row = np.concatenate([cosine, -sine_part], axis=1)
    imag_row = np.concatenate([sine_part, cosine], axis=1)
    table = np.stack([real_row, imag_row], axis=1).reshape(2 * pulses, 2 * pulses)
    return table.astype(ml_dtypes.bfloat16)


def beam_picks(beams):
    picks = np.zeros((2, GROUP * 2 * beams, 2 * beams), np.float32)
    for g in range(GROUP):
        for b in range(beams):
            re_row, im_row = g * 2 * beams + b, g * 2 * beams + beams + b
            picks[0, re_row, b] = 1
            picks[0, im_row, beams + b] = 1
            picks[1, re_row, beams + b] = -1
            picks[1, im_row, b] = 1
    return picks.astype(ml_dtypes.bfloat16)


def dot(a, b):
    return jnp.dot(a, b, preferred_element_type=F32)


def front_kernel(
    bins_chip, me_ref, order_ref, natural_ref, picks_ref, beam_ref, mine_ref, theirs_ref,
    send_ref, keep_ref, table_ref, weights_ref, spectra_ref,
):
    elem_dev = mine_ref.shape[0]
    groups = spectra_ref.shape[0]
    width = mine_ref.shape[-1]
    rows_in = natural_ref.shape[0]

    @pl.when(pl.program_id(0) == 0)
    def _():
        me = me_ref[0]
        order = order_ref[...]
        source = jnp.bitwise_xor(order[:, 0:1], me // 2) * (2 * bins_chip) + order[:, 1:2]
        source = lax.rem(source + rows_in, rows_in)
        lane = lax.broadcasted_iota(jnp.int32, (order.shape[0], rows_in), 1)
        picked = jnp.where(source == lane, 1.0, 0.0).astype(BF16)
        table_ref[...] = dot(picked, natural_ref[...]).astype(BF16)
        parts = beam_ref[...].astype(F32)
        parts = jnp.concatenate([parts[:, 0], parts[:, 1]], axis=0).astype(BF16)
        elements = parts.shape[1]
        columns = weights_ref.shape[1]
        row = lax.broadcasted_iota(jnp.int32, (elements, columns), 0)
        column = lax.broadcasted_iota(jnp.int32, (elements, columns), 1)
        held = column // (2 * GROUP)
        first = jnp.where(held < elem_dev, me, jnp.bitwise_xor(me, 1)) * elem_dev
        here = row == first + held % elem_dev
        total = jnp.zeros(weights_ref.shape, F32)
        for part in range(2):
            spread = jnp.where(here & (column % 2 == part), 1.0, 0.0).astype(BF16)
            total += dot(dot(picks_ref[part], parts).astype(BF16), spread)
        row = lax.broadcasted_iota(jnp.int32, weights_ref.shape, 0)
        column = lax.broadcasted_iota(jnp.int32, weights_ref.shape, 1)
        same = row // (weights_ref.shape[0] // GROUP) == column % (2 * GROUP) // 2
        weights_ref[...] = jnp.where(same, total, 0.0).astype(BF16)

    table = table_ref[...]
    for e in range(2 * elem_dev):
        spectra = dot(table, mine_ref[e] if e < elem_dev else theirs_ref[e - elem_dev])
        spectra_ref[:, e] = spectra.astype(BF16).reshape(groups, 2 * GROUP, width)
    weights = weights_ref[...]
    rows = weights.shape[0]
    for g in range(groups):
        sums = dot(weights, spectra_ref[g].reshape(-1, width))
        at = g % (groups // 2) * rows
        if g < groups // 2:
            keep_ref[at : at + rows] = sums
        else:
            send_ref[at : at + rows] = sums.astype(BF16)


def front(me, strides, extra, bins_chip, beam_weights, echo, theirs, start, width):
    elem_dev, rows_in, gate_count = echo.shape
    size = theirs.shape[2]
    beams = beam_weights.shape[0]
    order = row_order([s // 2 for s in strides], bins_chip, extra)
    natural = doppler_table(rows_in // 2)
    picks = beam_picks(beams)
    table_rows = order.shape[0]
    groups = table_rows // 2 // GROUP
    half = table_rows // 4 * 2 * beams
    first, across = start // width, gate_count // 2 // width
    block_rows, block_columns = GROUP * 2 * beams, elem_dev * 4 * GROUP
    whole = lambda shape: pl.BlockSpec(shape, lambda i, me: (0,) * len(shape))
    echo_block = (elem_dev, rows_in, width)
    return pl.pallas_call(
        functools.partial(front_kernel, bins_chip),
        grid_spec=pltpu.PrefetchScalarGridSpec(
            num_scalar_prefetch=1,
            grid=(size // width,),
            in_specs=[
                whole(order.shape),
                whole(natural.shape),
                whole(picks.shape),
                whole(beam_weights.shape),
                pl.BlockSpec(echo_block, lambda i, me: (0, 0, me[0] % 2 * across + first + i)),
                pl.BlockSpec(echo_block, lambda i, me: (0, 0, i)),
            ],
            out_specs=[
                pl.BlockSpec((half, width), lambda i, me: (0, i)),
                pl.BlockSpec((half, width), lambda i, me: (0, i)),
            ],
            scratch_shapes=[
                pltpu.VMEM((table_rows, rows_in), BF16),
                pltpu.VMEM((block_rows, block_columns), BF16),
                pltpu.VMEM((groups, 2 * elem_dev, 2 * GROUP, width), BF16),
            ],
        ),
        out_shape=[
            jax.ShapeDtypeStruct((half, size), BF16),
            jax.ShapeDtypeStruct((half, size), F32),
        ],
        compiler_params=pltpu.CompilerParams(vmem_limit_bytes=VMEM),
        cost_estimate=pl.CostEstimate(flops=1000, bytes_accessed=1000, transcendentals=0),
        name="front",
    )(me, jnp.asarray(order), jnp.asarray(natural), jnp.asarray(picks), beam_weights, echo, theirs)


def gram_sums(window, mask, rows):
    top = window.astype(BF16)
    rest = (window - top.astype(F32)).astype(BF16)
    picked_top, picked_rest = [], []
    for d in range(mask.shape[0]):
        keep = mask[d : d + 1].astype(F32).astype(BF16)
        picked_top.append(top[rows * d : rows * (d + 3)] * keep)
        picked_rest.append(rest[rows * d : rows * (d + 3)] * keep)
    left = jnp.concatenate(picked_top, axis=0)
    left_rest = jnp.concatenate(picked_rest, axis=0)
    dims = (((1,), (1,)), ((), ()))
    gram = lax.dot_general(left, top, dims, preferred_element_type=F32)
    gram += lax.dot_general(left, rest, dims, preferred_element_type=F32)
    gram += lax.dot_general(left_rest, top, dims, preferred_element_type=F32)
    return gram


def half_lanes(core, half, start, size):
    return lambda gates: pl.ds(pl.multiple_of((core ^ half) * (gates // 2) + start, 128), size)


def gram_kernel(spans, me_ref, edge_ref, mask_ref, *refs):
    parts, (gram_ref, window_ref) = refs[:-2], refs[-2:]
    rows = edge_ref.shape[0]
    inner = parts[0].shape[0]
    core = me_ref[0] % 2
    gates = mask_ref.shape[1]
    early = sum(size for _, size in spans)
    total = None
    for index, part in enumerate(parts):
        half, (start, size) = index // len(spans), spans[index % len(spans)]
        lanes = slice(start, start + size)
        inner_at = pl.multiple_of((1 - core) * rows, rows)
        edge_at = pl.multiple_of(core * inner, rows)
        window_ref[half, pl.ds(inner_at, inner), lanes] = part[...]
        edge = edge_ref[:, half * early + start : half * early + start + size]
        window_ref[half, pl.ds(edge_at, rows), lanes] = edge
        mask = mask_ref[:, half_lanes(core, half, start, size)(gates)]
        sums = gram_sums(window_ref[half, :, lanes], mask, rows)
        total = sums if total is None else total + sums
    gram_ref[...] = total


def gram_of(me, spans, mine, theirs, edge, mask):
    bins_here = mask.shape[0]
    rows = edge.shape[0]
    inner = mine[0].shape[0]
    early = sum(size for _, size in spans)
    return pl.pallas_call(
        functools.partial(gram_kernel, spans),
        in_specs=[pl.BlockSpec(memory_space=pltpu.SMEM)]
        + [pl.BlockSpec(memory_space=pltpu.VMEM)] * (2 + 2 * len(mine)),
        out_shape=[
            jax.ShapeDtypeStruct((bins_here * 3 * rows, inner + rows), F32),
            jax.ShapeDtypeStruct((2, inner + rows, early), F32),
        ],
        compiler_params=pltpu.CompilerParams(vmem_limit_bytes=VMEM),
        cost_estimate=pl.CostEstimate(flops=1000, bytes_accessed=1000, transcendentals=0),
        name="gram",
    )(me, edge, mask, *mine, *theirs)


def solve(gram, steer, bins_here, beams):
    rows, order = 2 * beams, 3 * beams
    lane = lax.broadcasted_iota(jnp.int32, (1, 1, 128), 2)
    real_lane = lane // beams % 2 == 0
    row_at = lax.broadcasted_iota(jnp.int32, (1, order, 128), 1)
    lane_at = lax.broadcasted_iota(jnp.int32, (1, order, 128), 2)
    diagonal = (lane_at // rows * beams + lane_at % beams == row_at) & (lane_at // beams % 2 == 0)
    diagonal &= lane_at < 3 * rows
    systems = []
    pad = jnp.zeros((3 * rows, 128 - 3 * rows), F32)
    for d in range(bins_here):
        block = gram[3 * rows * d : 3 * rows * (d + 1), rows * d : rows * (d + 3)]
        block = jnp.concatenate([block, pad], axis=1)
        pieces = [block[i : i + beams] for i in range(0, 3 * rows, beams)]
        from_re = jnp.concatenate(pieces[0::2], axis=0)
        from_im = jnp.concatenate(pieces[1::2], axis=0)
        real = from_re + pltpu.roll(from_im, 128 - beams, 1)
        imag = pltpu.roll(from_im, beams, 1) - from_re
        systems.append(jnp.where(real_lane[0], real, imag))
    system = jnp.stack(systems, axis=0)
    system = jnp.where(lane < 3 * rows, system, 0.0) + jnp.where(diagonal, LOADING, 0.0)
    pick = row_at[0, :, :order] == lane_at[0, :, :order]
    target_re = jnp.sum(jnp.where(pick, steer[0:1], 0.0), axis=1, keepdims=True)[None]
    target_im = jnp.sum(jnp.where(pick, steer[1:2], 0.0), axis=1, keepdims=True)[None]
    system = jnp.where(lane == 3 * rows, target_re, system)
    system = jnp.where(lane == 3 * rows + beams, target_im, system)

    def swapped(row):
        return jnp.where(real_lane, -pltpu.roll(row, 128 - beams, 2), pltpu.roll(row, beams, 2))

    for k in range(order):
        spot = k // beams * rows + k % beams
        pivot_row = system[:, k : k + 1, :]
        pivot_row = pivot_row / pivot_row[:, :, spot : spot + 1]
        factor_re = system[:, :, spot : spot + 1]
        factor_im = system[:, :, spot + beams : spot + beams + 1]
        changed = system - factor_re * pivot_row - factor_im * swapped(pivot_row)
        system = jnp.where(row_at == k, pivot_row, changed)

    solved_re = system[:, :, 3 * rows : 3 * rows + 1]
    solved_im = system[:, :, 3 * rows + beams : 3 * rows + beams + 1]
    response = jnp.sum(solved_re * target_re + solved_im * target_im, axis=1, keepdims=True)
    weight_re = jnp.broadcast_to(solved_re / response, (bins_here, order, 128))
    weight_im = jnp.broadcast_to(solved_im / response, (bins_here, order, 128))
    return weight_re, weight_im


def filter_gates(out_ref, at, blocks, weight_re, weight_im, beams):
    for d in range(weight_re.shape[0]):
        total_re = jnp.zeros((beams, 128), F32)
        total_im = jnp.zeros((beams, 128), F32)
        for w in range(3):
            coeff_re = weight_re[d, w * beams : (w + 1) * beams]
            coeff_im = weight_im[d, w * beams : (w + 1) * beams]
            snap_re, snap_im = blocks[2 * (d + w)], blocks[2 * (d + w) + 1]
            total_re += coeff_re * snap_re + coeff_im * snap_im
            total_im += coeff_re * snap_im - coeff_im * snap_re
        row_re = jnp.sum(total_re, axis=0, keepdims=True)
        row_im = jnp.sum(total_im, axis=0, keepdims=True)
        out_ref[d, :, at] = jnp.concatenate([row_re, row_im], axis=0)


def tail_kernel(me_ref, steer_ref, gram_ref, window_ref, mask_ref, *refs):
    parts, out_ref = refs[:-1], refs[-1]
    bins_here, gates = mask_ref.shape
    rows = window_ref.shape[1] // (bins_here + 2)
    beams = rows // 2
    core = me_ref[0] % 2
    pieces = [(0, 0, window_ref.at[0]), (1, 0, window_ref.at[1])]
    gram = gram_ref[...]
    count = len(parts) // 2
    for half in range(2):
        start = window_ref.shape[2]
        for ref in parts[half * count : (half + 1) * count]:
            size = ref.shape[1]
            mask = mask_ref[:, half_lanes(core, half, start, size)(gates)]
            gram += gram_sums(ref[...], mask, rows)
            pieces.append((half, start, ref))
            start += size
    weight_re, weight_im = solve(gram, steer_ref[...], bins_here, beams)

    def split(value):
        return [value[i : i + beams] for i in range(0, value.shape[0], beams)]

    for half, start, ref in pieces:
        for at in range(0, ref.shape[1], 128):
            lanes = half_lanes(core, half, start + at, 128)(gates)
            blocks = split(ref[:, at : at + 128])
            filter_gates(out_ref, lanes, blocks, weight_re, weight_im, beams)


def tail(me, steer, gram, window, mask, mine, theirs):
    bins_here, gates = mask.shape
    parts = mine + theirs
    return pl.pallas_call(
        tail_kernel,
        in_specs=[pl.BlockSpec(memory_space=pltpu.SMEM)]
        + [pl.BlockSpec(memory_space=pltpu.VMEM)] * (4 + len(parts)),
        out_shape=jax.ShapeDtypeStruct((bins_here, 2, gates), F32),
        compiler_params=pltpu.CompilerParams(vmem_limit_bytes=VMEM),
        cost_estimate=pl.CostEstimate(flops=1000, bytes_accessed=1000, transcendentals=0),
        name="tail",
    )(me, steer, gram, window, mask, *parts)


def slice_kernel(me_ref, echo_ref, part_ref):
    part_ref[...] = echo_ref[...]


def other_half(me, echo, start, size):
    elem_dev, rows_in, gate_count = echo.shape
    first, across = start // 128, gate_count // 2 // 128
    block = (elem_dev, rows_in, 128)
    return pl.pallas_call(
        slice_kernel,
        grid_spec=pltpu.PrefetchScalarGridSpec(
            num_scalar_prefetch=1,
            grid=(size // 128,),
            in_specs=[pl.BlockSpec(block, lambda i, me: (0, 0, (1 - me[0] % 2) * across + first + i))],
            out_specs=pl.BlockSpec(block, lambda i, me: (0, 0, i)),
        ),
        out_shape=jax.ShapeDtypeStruct((elem_dev, rows_in, size), BF16),
        compiler_params=pltpu.CompilerParams(vmem_limit_bytes=VMEM),
        cost_estimate=pl.CostEstimate(flops=1000, bytes_accessed=1000, transcendentals=0),
        name="slice",
    )(me, echo)


def swap(x, stride, count):
    return lax.ppermute(x, "elem", [(i, i ^ stride) for i in range(count)])


def share(keep, received, part):
    total = keep[part]
    for got in received:
        total = total + got[part].astype(F32)
    return total


class Chain:
    def __init__(self):
        self.last = None

    def enter(self, value):
        if self.last is None:
            return value
        value, _ = lax.optimization_barrier((value, self.last))
        return value

    def leave(self, value):
        self.last = value
        return value


def local(raw_echo, beam_weights, steer, train_mask):
    elem_dev, _, pulses, gate_count = raw_echo.shape
    count = lax.axis_size("elem")
    me = lax.axis_index("elem").astype(jnp.int32)
    core = me % 2
    at = me.reshape(1)
    bins_here = pulses // count
    rows = 2 * beam_weights.shape[0]
    echo = raw_echo.reshape(elem_dev, 2 * pulses, gate_count)
    levels = count.bit_length() - 1
    plain = [2 << i for i in range(levels - 1)]
    orders = [plain, plain[1:] + plain[:1]]
    unit = gate_count // 2 // sum(width for width, _, _ in CHUNKS)
    chunks = len(CHUNKS)
    last = sum(1 - wide for _, _, wide in CHUNKS)
    spans = []
    for width, _, _ in CHUNKS:
        start = sum(spans[-1]) if spans else 0
        spans.append((start, width * unit))
    early = tuple(spans[:last])
    theirs = [None] * chunks
    keeps, received = [None] * chunks, [[] for _ in CHUNKS]
    near, far = [None] * chunks, [None] * chunks
    chain = Chain()
    edge = gram = window = None

    steps = []
    for c, stage in STEPS:
        if stage == 3:
            steps += [(c, later) for later in range(3, levels)]
        else:
            steps.append((c, levels if stage == 4 else stage))
    for c, stage in steps:
        if c == "halo":
            edges = [
                lax.dynamic_slice_in_dim(x, core * bins_here * rows, rows, 0)
                for x in far[:last] + near[:last]
            ]
            pairs = [((i + 1) % count, i) for i in range(1, count, 2)]
            pairs += [(i, (i + 1) % count) for i in range(1, count, 2)]
            edge = lax.ppermute(jnp.concatenate(edges, axis=1), "elem", pairs)
        elif c == "gram":
            gram, window = gram_of(at, early, near[:last], far[:last], edge, chain.enter(train_mask))
            chain.leave(gram)
        elif stage == 0:
            part = chain.leave(other_half(at, chain.enter(echo), *spans[c]))
            theirs[c] = swap(part, 1, count)
        elif stage == 1:
            start, size = spans[c]
            strides = orders[CHUNKS[c][1]]
            width = math.gcd(size, start, gate_count // 2)
            send, keeps[c] = front(
                at, strides, CHUNKS[c][2], 2 * bins_here, beam_weights,
                chain.enter(echo), theirs[c], start, width,
            )
            chain.leave(send)
            received[c].append(swap(send, strides[0], count))
        elif stage < levels:
            half = keeps[c].shape[0] >> (stage - 1)
            total = share(chain.enter(keeps[c]), received[c], slice(half, 2 * half))
            send = chain.leave(total.astype(BF16))
            received[c].append(swap(send, orders[CHUNKS[c][1]][stage - 1], count))
        else:
            held = keeps[c].shape[0] >> (levels - 2)
            total = chain.leave(share(chain.enter(keeps[c]), received[c], slice(0, held)))
            step = (bins_here - 1 + CHUNKS[c][2]) * rows
            near[c] = lax.dynamic_slice_in_dim(total, core * step, held - step, 0)
            send = lax.dynamic_slice_in_dim(total, (1 - core) * step, held - step, 0)
            far[c] = swap(send, 1, count)
    return tail(at, steer, gram, window, train_mask, near[last:], far[last:])


def solution(mesh):
    return jax.shard_map(
        local,
        mesh=mesh,
        in_specs=(P(("cpi", "elem"), None, None, None), P(), P(), P(("cpi", "elem"), None)),
        out_specs=P(("cpi", "elem"), None, None),
        check_vma=False,
    )
```

```python
import functools
import math

import jax
import jax.numpy as jnp
import ml_dtypes
import numpy as np
from jax import lax
from jax.experimental import pallas as pl
from jax.experimental.pallas import tpu as pltpu
from jax.sharding import PartitionSpec as P

LOADING = 1.0
F32 = jnp.float32
BF16 = jnp.bfloat16
GROUP = 8
VMEM = 48 << 20
CHUNKS = ((2, 1, 0, 0), (3, 0, 0, 0), (3, 0, 0, 0), (2, 0, 1, 0), (2, 0, 1, 0))
AHEAD = 2
STEPS = (
    (1, 0), (2, 0), (1, 1), (2, 1), (0, 1), (1, 2), (0, 2), (4, 1), (3, 1), (1, 3),
    (0, 3), (2, 2), (2, 11), (2, 3), (3, 2), (4, 2), (0, 4), (1, 4), (2, 4), (3, 3),
    (4, 3), (3, 4), ("halo", 0), ("gram", 0), (4, 4),
)


def block_at(strides):
    count = len(strides)
    blocks = []
    for position in range(1 << count):
        blocks.append(sum(s for i, s in enumerate(strides) if position >> (count - 1 - i) & 1))
    return blocks


def row_order(strides, bins_here, extra):
    rows = []
    for block in block_at(strides):
        for j in range(-extra, bins_here + extra):
            rows += [(block, 2 * j), (block, 2 * j + 1)]
    return np.array(rows, np.int32)


def doppler_table(pulses):
    index = np.arange(pulses)
    angles = (-2.0 * math.pi / pulses * (index[:, None] * index[None, :] % pulses)).astype(np.float32)
    cosine = np.cos(angles) / np.float32(math.sqrt(pulses))
    sine_part = np.sin(angles) / np.float32(math.sqrt(pulses))
    real_row = np.concatenate([cosine, -sine_part], axis=1)
    imag_row = np.concatenate([sine_part, cosine], axis=1)
    table = np.stack([real_row, imag_row], axis=1).reshape(2 * pulses, 2 * pulses)
    return table.astype(ml_dtypes.bfloat16)


def beam_picks(beams):
    picks = np.zeros((2, GROUP * 2 * beams, 2 * beams), np.float32)
    for g in range(GROUP):
        for b in range(beams):
            re_row, im_row = g * 2 * beams + b, g * 2 * beams + beams + b
            picks[0, re_row, b] = 1
            picks[0, im_row, beams + b] = 1
            picks[1, re_row, beams + b] = -1
            picks[1, im_row, b] = 1
    return picks.astype(ml_dtypes.bfloat16)


def dot(a, b):
    return jnp.dot(a, b, preferred_element_type=F32)


def front_kernel(
    bins_chip, ahead, parts, me_ref, order_ref, natural_ref, picks_ref, beam_ref, mine_ref, theirs_ref, *refs
):
    if ahead:
        refs[2 + parts][...] = refs[0][...]
        refs = refs[1 : 2 + parts] + refs[3 + parts :]
    sends, keep_ref, table_ref, weights_ref, spectra_ref = refs[:parts], *refs[parts:]
    elem_dev = mine_ref.shape[0]
    groups = spectra_ref.shape[0]
    width = mine_ref.shape[-1]
    rows_in = natural_ref.shape[0]
    me = me_ref[0]
    order = order_ref[...]
    source = jnp.bitwise_xor(order[:, 0:1], me // 2) * (2 * bins_chip) + order[:, 1:2]
    source = lax.rem(source + rows_in, rows_in)
    lane = lax.broadcasted_iota(jnp.int32, (order.shape[0], rows_in), 1)
    picked = jnp.where(source == lane, 1.0, 0.0).astype(BF16)
    table_ref[...] = dot(picked, natural_ref[...]).astype(BF16)
    given = beam_ref[...].astype(F32)
    given = jnp.concatenate([given[:, 0], given[:, 1]], axis=0).astype(BF16)
    elements = given.shape[1]
    columns = weights_ref.shape[1]
    row = lax.broadcasted_iota(jnp.int32, (elements, columns), 0)
    column = lax.broadcasted_iota(jnp.int32, (elements, columns), 1)
    held = column // (2 * GROUP)
    first = jnp.where(held < elem_dev, me, jnp.bitwise_xor(me, 1)) * elem_dev
    here = row == first + held % elem_dev
    total = jnp.zeros(weights_ref.shape, F32)
    for part in range(2):
        spread = jnp.where(here & (column % 2 == part), 1.0, 0.0).astype(BF16)
        total += dot(dot(picks_ref[part], given).astype(BF16), spread)
    row = lax.broadcasted_iota(jnp.int32, weights_ref.shape, 0)
    column = lax.broadcasted_iota(jnp.int32, weights_ref.shape, 1)
    same = row // (weights_ref.shape[0] // GROUP) == column % (2 * GROUP) // 2
    weights_ref[...] = jnp.where(same, total, 0.0).astype(BF16)

    table = table_ref[...]
    for e in range(2 * elem_dev):
        spectra = dot(table, mine_ref[e] if e < elem_dev else theirs_ref[e - elem_dev])
        spectra_ref[:, e] = spectra.astype(BF16).reshape(groups, 2 * GROUP, width)
    weights = weights_ref[...]
    rows = weights.shape[0]
    tall = sends[0].shape[0]
    for g in range(groups):
        sums = dot(weights, spectra_ref[g].reshape(-1, width))
        if g < groups // 2:
            keep_ref[g * rows : (g + 1) * rows] = sums
            continue
        sums = sums.astype(BF16)
        for low in range(0, rows, 16):
            at = (g - groups // 2) * rows + low
            out_ref = sends[parts - 1 - at // tall]
            out_ref[at % tall : at % tall + 16] = sums[low : low + 16]


def front(me, strides, extra, bins_chip, beam_weights, echo, theirs, span, ahead, parts):
    elem_dev, rows_in, gate_count = echo.shape
    start, size = span
    beams = beam_weights.shape[0]
    order = row_order([s // 2 for s in strides], bins_chip, extra)
    natural = doppler_table(rows_in // 2)
    picks = beam_picks(beams)
    table_rows = order.shape[0]
    groups = table_rows // 2 // GROUP
    half = table_rows // 4 * 2 * beams
    block_rows, block_columns = GROUP * 2 * beams, elem_dev * 4 * GROUP
    whole = lambda shape: pl.BlockSpec(shape, lambda i, me: (0,) * len(shape))

    def gates(which, start, size):
        lane = lambda me: ((me[0] + which) % 2) * (gate_count // 2) + start
        return pl.BlockSpec(
            (pl.Element(elem_dev), pl.Element(rows_in), pl.Element(size)),
            lambda i, me: (0, 0, pl.multiple_of(lane(me), 128)),
        )

    in_specs = [whole(x.shape) for x in (order, natural, picks, beam_weights)]
    in_specs += [gates(0, start, size), whole(theirs.shape)]
    out_shape = [jax.ShapeDtypeStruct((half // parts, size), BF16)] * parts
    out_shape += [jax.ShapeDtypeStruct((half, size), F32)]
    operands = [me, jnp.asarray(order), jnp.asarray(natural), jnp.asarray(picks), beam_weights, echo, theirs]
    if ahead:
        in_specs.append(gates(1, *ahead))
        operands.append(echo)
        out_shape.append(jax.ShapeDtypeStruct((elem_dev, rows_in, ahead[1]), BF16))
    return pl.pallas_call(
        functools.partial(front_kernel, bins_chip, ahead is not None, parts),
        grid_spec=pltpu.PrefetchScalarGridSpec(
            num_scalar_prefetch=1,
            grid=(1,),
            in_specs=in_specs,
            out_specs=[whole(x.shape) for x in out_shape],
            scratch_shapes=[
                pltpu.VMEM((table_rows, rows_in), BF16),
                pltpu.VMEM((block_rows, block_columns), BF16),
                pltpu.VMEM((groups, 2 * elem_dev, 2 * GROUP, size), BF16),
            ],
        ),
        out_shape=out_shape,
        compiler_params=pltpu.CompilerParams(vmem_limit_bytes=VMEM),
        cost_estimate=pl.CostEstimate(flops=1000, bytes_accessed=1000, transcendentals=0),
        name="front",
    )(*operands)


def gram_sums(window, mask, rows):
    top = window.astype(BF16)
    rest = (window - top.astype(F32)).astype(BF16)
    picked_top, picked_rest = [], []
    for d in range(mask.shape[0]):
        keep = mask[d : d + 1].astype(F32).astype(BF16)
        picked_top.append(top[rows * d : rows * (d + 3)] * keep)
        picked_rest.append(rest[rows * d : rows * (d + 3)] * keep)
    left = jnp.concatenate(picked_top, axis=0)
    left_rest = jnp.concatenate(picked_rest, axis=0)
    dims = (((1,), (1,)), ((), ()))
    gram = lax.dot_general(left, top, dims, preferred_element_type=F32)
    gram += lax.dot_general(left, rest, dims, preferred_element_type=F32)
    gram += lax.dot_general(left_rest, top, dims, preferred_element_type=F32)
    return gram


def half_lanes(core, half, start, size):
    return lambda gates: pl.ds(pl.multiple_of((core ^ half) * (gates // 2) + start, 128), size)


def gram_kernel(spans, me_ref, edge_ref, mask_ref, *refs):
    parts, (gram_ref, window_ref) = refs[:-2], refs[-2:]
    rows = edge_ref.shape[0]
    inner = parts[0].shape[0]
    core = me_ref[0] % 2
    gates = mask_ref.shape[1]
    early = sum(size for _, size in spans)
    total = None
    for index, part in enumerate(parts):
        half, (start, size) = index // len(spans), spans[index % len(spans)]
        lanes = slice(start, start + size)
        inner_at = pl.multiple_of((1 - core) * rows, rows)
        edge_at = pl.multiple_of(core * inner, rows)
        window_ref[half, pl.ds(inner_at, inner), lanes] = part[...]
        edge = edge_ref[:, half * early + start : half * early + start + size]
        window_ref[half, pl.ds(edge_at, rows), lanes] = edge
        mask = mask_ref[:, half_lanes(core, half, start, size)(gates)]
        sums = gram_sums(window_ref[half, :, lanes], mask, rows)
        total = sums if total is None else total + sums
    gram_ref[...] = total


def gram_of(me, spans, mine, theirs, edge, mask):
    bins_here = mask.shape[0]
    rows = edge.shape[0]
    inner = mine[0].shape[0]
    early = sum(size for _, size in spans)
    return pl.pallas_call(
        functools.partial(gram_kernel, spans),
        in_specs=[pl.BlockSpec(memory_space=pltpu.SMEM)]
        + [pl.BlockSpec(memory_space=pltpu.VMEM)] * (2 + 2 * len(mine)),
        out_shape=[
            jax.ShapeDtypeStruct((bins_here * 3 * rows, inner + rows), F32),
            jax.ShapeDtypeStruct((2, inner + rows, early), F32),
        ],
        compiler_params=pltpu.CompilerParams(vmem_limit_bytes=VMEM),
        cost_estimate=pl.CostEstimate(flops=1000, bytes_accessed=1000, transcendentals=0),
        name="gram",
    )(me, edge, mask, *mine, *theirs)


def solve(gram, steer, bins_here, beams):
    rows, order = 2 * beams, 3 * beams
    lane = lax.broadcasted_iota(jnp.int32, (1, 1, 128), 2)
    real_lane = lane // beams % 2 == 0
    row_at = lax.broadcasted_iota(jnp.int32, (1, order, 128), 1)
    lane_at = lax.broadcasted_iota(jnp.int32, (1, order, 128), 2)
    diagonal = (lane_at // rows * beams + lane_at % beams == row_at) & (lane_at // beams % 2 == 0)
    diagonal &= lane_at < 3 * rows
    systems = []
    pad = jnp.zeros((3 * rows, 128 - 3 * rows), F32)
    for d in range(bins_here):
        block = gram[3 * rows * d : 3 * rows * (d + 1), rows * d : rows * (d + 3)]
        block = jnp.concatenate([block, pad], axis=1)
        pieces = [block[i : i + beams] for i in range(0, 3 * rows, beams)]
        from_re = jnp.concatenate(pieces[0::2], axis=0)
        from_im = jnp.concatenate(pieces[1::2], axis=0)
        real = from_re + pltpu.roll(from_im, 128 - beams, 1)
        imag = pltpu.roll(from_im, beams, 1) - from_re
        systems.append(jnp.where(real_lane[0], real, imag))
    system = jnp.stack(systems, axis=0)
    system = jnp.where(lane < 3 * rows, system, 0.0) + jnp.where(diagonal, LOADING, 0.0)
    pick = row_at[0, :, :order] == lane_at[0, :, :order]
    target_re = jnp.sum(jnp.where(pick, steer[0:1], 0.0), axis=1, keepdims=True)[None]
    target_im = jnp.sum(jnp.where(pick, steer[1:2], 0.0), axis=1, keepdims=True)[None]
    system = jnp.where(lane == 3 * rows, target_re, system)
    system = jnp.where(lane == 3 * rows + beams, target_im, system)

    def swapped(row):
        return jnp.where(real_lane, -pltpu.roll(row, 128 - beams, 2), pltpu.roll(row, beams, 2))

    for k in range(order):
        spot = k // beams * rows + k % beams
        pivot_row = system[:, k : k + 1, :]
        turned = swapped(pivot_row)
        pivot = jnp.broadcast_to(pivot_row[:, :, spot : spot + 1], pivot_row.shape)
        factor_re = system[:, :, spot : spot + 1]
        factor_im = system[:, :, spot + beams : spot + beams + 1]
        scale = 1.0 / pivot
        pivot_row = pivot_row * scale
        changed = system - factor_re * pivot_row - factor_im * (turned * scale)
        system = jnp.where(row_at == k, pivot_row, changed)

    solved_re = system[:, :, 3 * rows : 3 * rows + 1]
    solved_im = system[:, :, 3 * rows + beams : 3 * rows + beams + 1]
    response = jnp.sum(solved_re * target_re + solved_im * target_im, axis=1, keepdims=True)
    weight_re = jnp.broadcast_to(solved_re / response, (bins_here, order, 128))
    weight_im = jnp.broadcast_to(solved_im / response, (bins_here, order, 128))
    return weight_re, weight_im


def filter_gates(out_ref, at, blocks, weight_re, weight_im, beams):
    for d in range(weight_re.shape[0]):
        total_re = jnp.zeros((beams, 128), F32)
        total_im = jnp.zeros((beams, 128), F32)
        for w in range(3):
            coeff_re = weight_re[d, w * beams : (w + 1) * beams]
            coeff_im = weight_im[d, w * beams : (w + 1) * beams]
            snap_re, snap_im = blocks[2 * (d + w)], blocks[2 * (d + w) + 1]
            total_re += coeff_re * snap_re + coeff_im * snap_im
            total_im += coeff_re * snap_im - coeff_im * snap_re
        row_re = jnp.sum(total_re, axis=0, keepdims=True)
        row_im = jnp.sum(total_im, axis=0, keepdims=True)
        out_ref[d, :, at] = jnp.concatenate([row_re, row_im], axis=0)


def tail_kernel(me_ref, steer_ref, gram_ref, window_ref, mask_ref, *refs):
    parts, out_ref = refs[:-1], refs[-1]
    bins_here, gates = mask_ref.shape
    rows = window_ref.shape[1] // (bins_here + 2)
    beams = rows // 2
    core = me_ref[0] % 2
    pieces = [(0, 0, window_ref.at[0]), (1, 0, window_ref.at[1])]
    gram = gram_ref[...]
    count = len(parts) // 2
    for half in range(2):
        start = window_ref.shape[2]
        for ref in parts[half * count : (half + 1) * count]:
            size = ref.shape[1]
            mask = mask_ref[:, half_lanes(core, half, start, size)(gates)]
            gram += gram_sums(ref[...], mask, rows)
            pieces.append((half, start, ref))
            start += size
    weight_re, weight_im = solve(gram, steer_ref[...], bins_here, beams)

    def split(value):
        return [value[i : i + beams] for i in range(0, value.shape[0], beams)]

    for half, start, ref in pieces:
        for at in range(0, ref.shape[1], 128):
            lanes = half_lanes(core, half, start + at, 128)(gates)
            blocks = split(ref[:, at : at + 128])
            filter_gates(out_ref, lanes, blocks, weight_re, weight_im, beams)


def tail(me, steer, gram, window, mask, mine, theirs):
    bins_here, gates = mask.shape
    parts = mine + theirs
    return pl.pallas_call(
        tail_kernel,
        in_specs=[pl.BlockSpec(memory_space=pltpu.SMEM)]
        + [pl.BlockSpec(memory_space=pltpu.VMEM)] * (4 + len(parts)),
        out_shape=jax.ShapeDtypeStruct((bins_here, 2, gates), F32),
        compiler_params=pltpu.CompilerParams(vmem_limit_bytes=VMEM),
        cost_estimate=pl.CostEstimate(flops=1000, bytes_accessed=1000, transcendentals=0),
        name="tail",
    )(me, steer, gram, window, mask, *parts)


def slice_kernel(me_ref, echo_ref, part_ref):
    part_ref[...] = echo_ref[...]


def other_half(me, echo, start, size):
    elem_dev, rows_in, gate_count = echo.shape
    first, across = start // 128, gate_count // 2 // 128
    block = (elem_dev, rows_in, 128)
    return pl.pallas_call(
        slice_kernel,
        grid_spec=pltpu.PrefetchScalarGridSpec(
            num_scalar_prefetch=1,
            grid=(size // 128,),
            in_specs=[pl.BlockSpec(block, lambda i, me: (0, 0, (1 - me[0] % 2) * across + first + i))],
            out_specs=pl.BlockSpec(block, lambda i, me: (0, 0, i)),
        ),
        out_shape=jax.ShapeDtypeStruct((elem_dev, rows_in, size), BF16),
        compiler_params=pltpu.CompilerParams(vmem_limit_bytes=VMEM),
        cost_estimate=pl.CostEstimate(flops=1000, bytes_accessed=1000, transcendentals=0),
        name="slice",
    )(me, echo)


def swap(x, stride, count):
    return lax.ppermute(x, "elem", [(i, i ^ stride) for i in range(count)])


def share_kernel(count, keep_ref, *refs):
    received, sends = refs[:count], refs[count:]
    total = keep_ref[...]
    for got in received:
        total = total + got[...].astype(F32)
    total = total.astype(BF16)
    tall = sends[0].shape[0]
    for i, out_ref in enumerate(reversed(sends)):
        out_ref[...] = total[i * tall : (i + 1) * tall]


def share(keep, received, height, parts):
    size = keep.shape[1]
    block = (height, size)
    second = pl.BlockSpec(block, lambda i: (1, 0))
    operands, specs = [keep], [second]
    for got in received[:-1]:
        operands.append(got[-1])
        specs.append(second)
    operands.append(received[-1][0])
    specs.append(second if len(received[-1]) == 1 else pl.BlockSpec(block, lambda i: (0, 0)))
    return pl.pallas_call(
        functools.partial(share_kernel, len(received)),
        grid=(1,),
        in_specs=specs,
        out_specs=[pl.BlockSpec((height // parts, size), lambda i: (0, 0))] * parts,
        out_shape=[jax.ShapeDtypeStruct((height // parts, size), BF16)] * parts,
        compiler_params=pltpu.CompilerParams(vmem_limit_bytes=VMEM),
        cost_estimate=pl.CostEstimate(flops=1000, bytes_accessed=1000, transcendentals=0),
        name="share",
    )(*operands)


def finish_kernel(step, me_ref, keep_ref, *refs):
    received, near_ref, send_ref, total_ref = refs[:-3], *refs[-3:]
    total = keep_ref[...]
    for got in received:
        total = total + got[...].astype(F32)
    total_ref[...] = total
    core = me_ref[0] % 2
    height = near_ref.shape[0]
    near_ref[...] = total_ref[pl.ds(pl.multiple_of(core * step, 8), height)]
    send_ref[...] = total_ref[pl.ds(pl.multiple_of((1 - core) * step, 8), height)]


def finish(me, keep, received, held, step):
    size = keep.shape[1]
    part = pl.BlockSpec((held, size), lambda i: (0, 0))
    out = pl.BlockSpec((held - step, size), lambda i: (0, 0))
    return pl.pallas_call(
        functools.partial(finish_kernel, step),
        grid=(1,),
        in_specs=[pl.BlockSpec(memory_space=pltpu.SMEM)] + [part] * (1 + len(received)),
        out_specs=[out, out],
        out_shape=[jax.ShapeDtypeStruct((held - step, size), F32)] * 2,
        scratch_shapes=[pltpu.VMEM((held, size), F32)],
        compiler_params=pltpu.CompilerParams(vmem_limit_bytes=VMEM),
        cost_estimate=pl.CostEstimate(flops=1000, bytes_accessed=1000, transcendentals=0),
        name="finish",
    )(me, keep, *received)


def edges_kernel(rows, step, me_ref, *refs):
    parts, out_ref = refs[:-1], refs[-1]
    first = pl.multiple_of(me_ref[0] % 2 * step, 8)
    start = 0
    for part in parts:
        size = part.shape[1]
        out_ref[:, start : start + size] = part[pl.ds(first, rows)]
        start += size


def edges(me, parts, rows):
    width = sum(x.shape[1] for x in parts)
    return pl.pallas_call(
        functools.partial(edges_kernel, rows, parts[0].shape[0] - rows),
        in_specs=[pl.BlockSpec(memory_space=pltpu.SMEM)]
        + [pl.BlockSpec(memory_space=pltpu.VMEM)] * len(parts),
        out_shape=jax.ShapeDtypeStruct((rows, width), F32),
        compiler_params=pltpu.CompilerParams(vmem_limit_bytes=VMEM),
        cost_estimate=pl.CostEstimate(flops=1000, bytes_accessed=1000, transcendentals=0),
        name="edges",
    )(me, *parts)


class Chain:
    def __init__(self):
        self.last = None

    def enter(self, value):
        if self.last is None:
            return value
        value, _ = lax.optimization_barrier((value, self.last))
        return value

    def leave(self, value):
        self.last = value
        return value


def local(raw_echo, beam_weights, steer, train_mask):
    elem_dev, _, pulses, gate_count = raw_echo.shape
    count = lax.axis_size("elem")
    me = lax.axis_index("elem").astype(jnp.int32)
    at = me.reshape(1)
    bins_here = pulses // count
    rows = 2 * beam_weights.shape[0]
    echo = raw_echo.reshape(elem_dev, 2 * pulses, gate_count)
    levels = count.bit_length() - 1
    plain = [2 << i for i in range(levels - 1)]
    orders = [plain, plain[1:] + plain[:1], [plain[1], plain[0]] + plain[2:]]
    unit = gate_count // 2 // sum(width for width, _, _, _ in CHUNKS)
    chunks = len(CHUNKS)
    last = sum(1 - wide for _, _, wide, _ in CHUNKS)
    spans = []
    for width, _, _, _ in CHUNKS:
        start = sum(spans[-1]) if spans else 0
        spans.append((start, width * unit))
    early = tuple(spans[:last])
    theirs = [None] * chunks
    keeps, received = [None] * chunks, [[] for _ in CHUNKS]
    near, far = [None] * chunks, [None] * chunks
    chain = Chain()
    edge = gram = window = None

    steps = []
    for c, stage in STEPS:
        if stage == 3:
            steps += [(c, later) for later in range(3, levels)]
        else:
            steps.append((c, levels if stage == 4 else stage))
    turns = [c for c, stage in steps if stage == 1]
    for c, stage in steps:
        if c == "halo":
            out = edges(at, far[:last] + near[:last], rows)
            pairs = [((i + 1) % count, i) for i in range(1, count, 2)]
            pairs += [(i, (i + 1) % count) for i in range(1, count, 2)]
            edge = lax.ppermute(out, "elem", pairs)
        elif c == "gram":
            gram, window = gram_of(at, early, near[:last], far[:last], edge, chain.enter(train_mask))
            chain.leave(gram)
        elif stage == 0:
            part = chain.leave(other_half(at, chain.enter(echo), *spans[c]))
            theirs[c] = swap(part, 1, count)
        elif stage >= 10:
            got = received[c][stage - 10]
            got[0] = chain.leave(chain.enter(got[0]))
        elif stage == 1:
            strides = orders[CHUNKS[c][1]]
            later = turns.index(c) + AHEAD
            later = turns[later] if later < chunks else None
            parts = 1 + CHUNKS[c][3]
            out = front(
                at, strides, CHUNKS[c][2], 2 * bins_here, beam_weights,
                chain.enter(echo), theirs[c], spans[c], None if later is None else spans[later], parts,
            )
            send, keeps[c], part = out[:parts], out[parts], out[parts + 1 :]
            if part:
                theirs[later] = swap(part[0], 1, count)
            chain.leave(send[0])
            received[c].append([swap(x, strides[0], count) for x in send])
        elif stage < levels:
            half = keeps[c].shape[0] >> (stage - 1)
            parts = 1 + CHUNKS[c][3] * (stage < levels - 1)
            send = share(chain.enter(keeps[c]), received[c], half, parts)
            chain.leave(send[0])
            received[c].append([swap(x, orders[CHUNKS[c][1]][stage - 1], count) for x in send])
        else:
            held = keeps[c].shape[0] >> (levels - 2)
            step = (bins_here - 1 + CHUNKS[c][2]) * rows
            near[c], send = finish(at, chain.enter(keeps[c]), [x[-1] for x in received[c]], held, step)
            chain.leave(send)
            far[c] = swap(send, 1, count)
    return tail(at, steer, gram, window, train_mask, near[last:], far[last:])


def solution(mesh):
    return jax.shard_map(
        local,
        mesh=mesh,
        in_specs=(P(("cpi", "elem"), None, None, None), P(), P(), P(("cpi", "elem"), None)),
        out_specs=P(("cpi", "elem"), None, None),
        check_vma=False,
    )
```

```python
import functools
import math

import jax
import jax.numpy as jnp
import ml_dtypes
import numpy as np
from jax import lax
from jax.experimental import pallas as pl
from jax.experimental.pallas import tpu as pltpu
from jax.sharding import PartitionSpec as P

LOADING = 1.0
F32 = jnp.float32
BF16 = jnp.bfloat16
GROUP = 8
VMEM = 48 << 20
CHUNKS = ((2, 1, 0, 0), (3, 0, 0, 0), (3, 0, 0, 0), (2, 0, 1, 0), (2, 0, 1, 0))
AHEAD = 2
STEPS = (
    (1, 0), (2, 0), (1, 1), (2, 1), (0, 1), (1, 2), (0, 2), (4, 1), (3, 1), (1, 3),
    (0, 3), (2, 2), (2, 11), (2, 3), (3, 2), (4, 2), (0, 4), (1, 4), (2, 4), (3, 3),
    (4, 3), (3, 4), ("halo", 0), ("gram", 0), (4, 4),
)


def block_at(strides):
    count = len(strides)
    blocks = []
    for position in range(1 << count):
        blocks.append(sum(s for i, s in enumerate(strides) if position >> (count - 1 - i) & 1))
    return blocks


def row_order(strides, bins_here, extra):
    rows = []
    for block in block_at(strides):
        for j in range(-extra, bins_here + extra):
            rows += [(block, 2 * j), (block, 2 * j + 1)]
    return np.array(rows, np.int32)


def doppler_table(pulses):
    index = np.arange(pulses)
    angles = (-2.0 * math.pi / pulses * (index[:, None] * index[None, :] % pulses)).astype(np.float32)
    cosine = np.cos(angles) / np.float32(math.sqrt(pulses))
    sine_part = np.sin(angles) / np.float32(math.sqrt(pulses))
    real_row = np.concatenate([cosine, -sine_part], axis=1)
    imag_row = np.concatenate([sine_part, cosine], axis=1)
    table = np.stack([real_row, imag_row], axis=1).reshape(2 * pulses, 2 * pulses)
    return table.astype(ml_dtypes.bfloat16)


def beam_picks(beams):
    picks = np.zeros((2, GROUP * 2 * beams, 2 * beams), np.float32)
    for g in range(GROUP):
        for b in range(beams):
            re_row, im_row = g * 2 * beams + b, g * 2 * beams + beams + b
            picks[0, re_row, b] = 1
            picks[0, im_row, beams + b] = 1
            picks[1, re_row, beams + b] = -1
            picks[1, im_row, b] = 1
    return picks.astype(ml_dtypes.bfloat16)


def dot(a, b):
    return jnp.dot(a, b, preferred_element_type=F32)


def front_kernel(
    bins_chip, ahead, parts, me_ref, order_ref, natural_ref, picks_ref, beam_ref, mine_ref, theirs_ref, *refs
):
    if ahead:
        refs[2 + parts][...] = refs[0][...]
        refs = refs[1 : 2 + parts] + refs[3 + parts :]
    sends, keep_ref, table_ref, weights_ref, spectra_ref = refs[:parts], *refs[parts:]
    elem_dev = mine_ref.shape[0]
    groups = spectra_ref.shape[0]
    width = mine_ref.shape[-1]
    rows_in = natural_ref.shape[0]
    me = me_ref[0]
    order = order_ref[...]
    source = jnp.bitwise_xor(order[:, 0:1], me // 2) * (2 * bins_chip) + order[:, 1:2]
    source = lax.rem(source + rows_in, rows_in)
    lane = lax.broadcasted_iota(jnp.int32, (order.shape[0], rows_in), 1)
    picked = jnp.where(source == lane, 1.0, 0.0).astype(BF16)
    table_ref[...] = dot(picked, natural_ref[...]).astype(BF16)
    given = beam_ref[...].astype(F32)
    given = jnp.concatenate([given[:, 0], given[:, 1]], axis=0).astype(BF16)
    elements = given.shape[1]
    columns = weights_ref.shape[1]
    row = lax.broadcasted_iota(jnp.int32, (elements, columns), 0)
    column = lax.broadcasted_iota(jnp.int32, (elements, columns), 1)
    held = column // (2 * GROUP)
    first = jnp.where(held < elem_dev, me, jnp.bitwise_xor(me, 1)) * elem_dev
    here = row == first + held % elem_dev
    total = jnp.zeros(weights_ref.shape, F32)
    for part in range(2):
        spread = jnp.where(here & (column % 2 == part), 1.0, 0.0).astype(BF16)
        total += dot(dot(picks_ref[part], given).astype(BF16), spread)
    row = lax.broadcasted_iota(jnp.int32, weights_ref.shape, 0)
    column = lax.broadcasted_iota(jnp.int32, weights_ref.shape, 1)
    same = row // (weights_ref.shape[0] // GROUP) == column % (2 * GROUP) // 2
    weights_ref[...] = jnp.where(same, total, 0.0).astype(BF16)

    table = table_ref[...]
    for e in range(2 * elem_dev):
        spectra = dot(table, mine_ref[e] if e < elem_dev else theirs_ref[e - elem_dev])
        spectra_ref[:, e] = spectra.astype(BF16).reshape(groups, 2 * GROUP, width)
    weights = weights_ref[...]
    rows = weights.shape[0]
    tall = sends[0].shape[0]
    for g in range(groups):
        sums = dot(weights, spectra_ref[g].reshape(-1, width))
        if g < groups // 2:
            keep_ref[g * rows : (g + 1) * rows] = sums
            continue
        sums = sums.astype(BF16)
        for low in range(0, rows, 16):
            at = (g - groups // 2) * rows + low
            out_ref = sends[parts - 1 - at // tall]
            out_ref[at % tall : at % tall + 16] = sums[low : low + 16]


def front(me, strides, extra, bins_chip, beam_weights, echo, theirs, span, ahead, parts):
    elem_dev, rows_in, gate_count = echo.shape
    start, size = span
    beams = beam_weights.shape[0]
    order = row_order([s // 2 for s in strides], bins_chip, extra)
    natural = doppler_table(rows_in // 2)
    picks = beam_picks(beams)
    table_rows = order.shape[0]
    groups = table_rows // 2 // GROUP
    half = table_rows // 4 * 2 * beams
    block_rows, block_columns = GROUP * 2 * beams, elem_dev * 4 * GROUP
    whole = lambda shape: pl.BlockSpec(shape, lambda i, me: (0,) * len(shape))

    def gates(which, start, size):
        lane = lambda me: ((me[0] + which) % 2) * (gate_count // 2) + start
        return pl.BlockSpec(
            (pl.Element(elem_dev), pl.Element(rows_in), pl.Element(size)),
            lambda i, me: (0, 0, pl.multiple_of(lane(me), 128)),
        )

    in_specs = [whole(x.shape) for x in (order, natural, picks, beam_weights)]
    in_specs += [gates(0, start, size), whole(theirs.shape)]
    out_shape = [jax.ShapeDtypeStruct((half // parts, size), BF16)] * parts
    out_shape += [jax.ShapeDtypeStruct((half, size), F32)]
    operands = [me, jnp.asarray(order), jnp.asarray(natural), jnp.asarray(picks), beam_weights, echo, theirs]
    if ahead:
        in_specs.append(gates(1, *ahead))
        operands.append(echo)
        out_shape.append(jax.ShapeDtypeStruct((elem_dev, rows_in, ahead[1]), BF16))
    return pl.pallas_call(
        functools.partial(front_kernel, bins_chip, ahead is not None, parts),
        grid_spec=pltpu.PrefetchScalarGridSpec(
            num_scalar_prefetch=1,
            grid=(1,),
            in_specs=in_specs,
            out_specs=[whole(x.shape) for x in out_shape],
            scratch_shapes=[
                pltpu.VMEM((table_rows, rows_in), BF16),
                pltpu.VMEM((block_rows, block_columns), BF16),
                pltpu.VMEM((groups, 2 * elem_dev, 2 * GROUP, size), BF16),
            ],
        ),
        out_shape=out_shape,
        compiler_params=pltpu.CompilerParams(vmem_limit_bytes=VMEM),
        cost_estimate=pl.CostEstimate(flops=1000, bytes_accessed=1000, transcendentals=0),
        name="front",
    )(*operands)


def gram_sums(window, mask, rows):
    top = window.astype(BF16)
    rest = (window - top.astype(F32)).astype(BF16)
    picked_top, picked_rest = [], []
    for d in range(mask.shape[0]):
        keep = mask[d : d + 1].astype(F32).astype(BF16)
        picked_top.append(top[rows * d : rows * (d + 3)] * keep)
        picked_rest.append(rest[rows * d : rows * (d + 3)] * keep)
    left = jnp.concatenate(picked_top, axis=0)
    left_rest = jnp.concatenate(picked_rest, axis=0)
    dims = (((1,), (1,)), ((), ()))
    gram = lax.dot_general(left, top, dims, preferred_element_type=F32)
    gram += lax.dot_general(left, rest, dims, preferred_element_type=F32)
    gram += lax.dot_general(left_rest, top, dims, preferred_element_type=F32)
    return gram


def half_lanes(core, half, start, size):
    return lambda gates: pl.ds(pl.multiple_of((core ^ half) * (gates // 2) + start, 128), size)


def gram_kernel(spans, me_ref, edge_ref, mask_ref, *refs):
    parts, (gram_ref, window_ref) = refs[:-2], refs[-2:]
    rows = edge_ref.shape[0]
    inner = parts[0].shape[0]
    core = me_ref[0] % 2
    gates = mask_ref.shape[1]
    early = sum(size for _, size in spans)
    total = None
    for index, part in enumerate(parts):
        half, (start, size) = index // len(spans), spans[index % len(spans)]
        lanes = slice(start, start + size)
        inner_at = pl.multiple_of((1 - core) * rows, rows)
        edge_at = pl.multiple_of(core * inner, rows)
        window_ref[half, pl.ds(inner_at, inner), lanes] = part[...]
        edge = edge_ref[:, half * early + start : half * early + start + size]
        window_ref[half, pl.ds(edge_at, rows), lanes] = edge
        mask = mask_ref[:, half_lanes(core, half, start, size)(gates)]
        sums = gram_sums(window_ref[half, :, lanes], mask, rows)
        total = sums if total is None else total + sums
    gram_ref[...] = total


def gram_of(me, spans, mine, theirs, edge, mask):
    bins_here = mask.shape[0]
    rows = edge.shape[0]
    inner = mine[0].shape[0]
    early = sum(size for _, size in spans)
    return pl.pallas_call(
        functools.partial(gram_kernel, spans),
        in_specs=[pl.BlockSpec(memory_space=pltpu.SMEM)]
        + [pl.BlockSpec(memory_space=pltpu.VMEM)] * (2 + 2 * len(mine)),
        out_shape=[
            jax.ShapeDtypeStruct((bins_here * 3 * rows, inner + rows), F32),
            jax.ShapeDtypeStruct((2, inner + rows, early), F32),
        ],
        compiler_params=pltpu.CompilerParams(vmem_limit_bytes=VMEM),
        cost_estimate=pl.CostEstimate(flops=1000, bytes_accessed=1000, transcendentals=0),
        name="gram",
    )(me, edge, mask, *mine, *theirs)


def solve(gram, steer, bins_here, beams):
    rows, order = 2 * beams, 3 * beams
    lane = lax.broadcasted_iota(jnp.int32, (1, 1, 128), 2)
    real_lane = lane // beams % 2 == 0
    row_at = lax.broadcasted_iota(jnp.int32, (1, order, 128), 1)
    lane_at = lax.broadcasted_iota(jnp.int32, (1, order, 128), 2)
    diagonal = (lane_at // rows * beams + lane_at % beams == row_at) & (lane_at // beams % 2 == 0)
    diagonal &= lane_at < 3 * rows
    systems = []
    pad = jnp.zeros((3 * rows, 128 - 3 * rows), F32)
    for d in range(bins_here):
        block = gram[3 * rows * d : 3 * rows * (d + 1), rows * d : rows * (d + 3)]
        block = jnp.concatenate([block, pad], axis=1)
        pieces = [block[i : i + beams] for i in range(0, 3 * rows, beams)]
        from_re = jnp.concatenate(pieces[0::2], axis=0)
        from_im = jnp.concatenate(pieces[1::2], axis=0)
        real = from_re + pltpu.roll(from_im, 128 - beams, 1)
        imag = pltpu.roll(from_im, beams, 1) - from_re
        systems.append(jnp.where(real_lane[0], real, imag))
    system = jnp.stack(systems, axis=0)
    system = jnp.where(lane < 3 * rows, system, 0.0) + jnp.where(diagonal, LOADING, 0.0)
    pick = row_at[0, :, :order] == lane_at[0, :, :order]
    target_re = jnp.sum(jnp.where(pick, steer[0:1], 0.0), axis=1, keepdims=True)[None]
    target_im = jnp.sum(jnp.where(pick, steer[1:2], 0.0), axis=1, keepdims=True)[None]
    system = jnp.where(lane == 3 * rows, target_re, system)
    system = jnp.where(lane == 3 * rows + beams, target_im, system)

    def swapped(row):
        return jnp.where(real_lane[0], -pltpu.roll(row, 128 - beams, 1), pltpu.roll(row, beams, 1))

    across = jnp.transpose(system, (1, 0, 2))
    held = [across[i] for i in range(order)]
    for k in range(order):
        spot = k // beams * rows + k % beams
        pivot_row = held[k]
        turned = swapped(pivot_row)
        scale = 1.0 / jnp.broadcast_to(pivot_row[:, spot : spot + 1], pivot_row.shape)
        pivot_row, turned = pivot_row * scale, turned * scale
        for i in range(order):
            if i != k:
                factor_re = held[i][:, spot : spot + 1]
                factor_im = held[i][:, spot + beams : spot + beams + 1]
                held[i] = held[i] - factor_re * pivot_row - factor_im * turned
        held[k] = pivot_row

    solved_re = [row[:, 3 * rows : 3 * rows + 1] for row in held]
    solved_im = [row[:, 3 * rows + beams : 3 * rows + beams + 1] for row in held]
    response = jnp.zeros((bins_here, 1), F32)
    for i in range(order):
        response += solved_re[i] * target_re[0, i : i + 1] + solved_im[i] * target_im[0, i : i + 1]
    scale = 1.0 / jnp.broadcast_to(response, (bins_here, 128))
    weight_re = jnp.stack([part * scale for part in solved_re], axis=0)
    weight_im = jnp.stack([part * scale for part in solved_im], axis=0)
    return jnp.transpose(weight_re, (1, 0, 2)), jnp.transpose(weight_im, (1, 0, 2))


def filter_gates(out_ref, at, blocks, weight_re, weight_im, beams):
    for d in range(weight_re.shape[0]):
        total_re = jnp.zeros((beams, 128), F32)
        total_im = jnp.zeros((beams, 128), F32)
        for w in range(3):
            coeff_re = weight_re[d, w * beams : (w + 1) * beams]
            coeff_im = weight_im[d, w * beams : (w + 1) * beams]
            snap_re, snap_im = blocks[2 * (d + w)], blocks[2 * (d + w) + 1]
            total_re += coeff_re * snap_re + coeff_im * snap_im
            total_im += coeff_re * snap_im - coeff_im * snap_re
        row_re = jnp.sum(total_re, axis=0, keepdims=True)
        row_im = jnp.sum(total_im, axis=0, keepdims=True)
        out_ref[d, :, at] = jnp.concatenate([row_re, row_im], axis=0)


def tail_kernel(me_ref, steer_ref, gram_ref, window_ref, mask_ref, *refs):
    parts, out_ref = refs[:-1], refs[-1]
    bins_here, gates = mask_ref.shape
    rows = window_ref.shape[1] // (bins_here + 2)
    beams = rows // 2
    core = me_ref[0] % 2
    pieces = [(0, 0, window_ref.at[0]), (1, 0, window_ref.at[1])]
    gram = gram_ref[...]
    count = len(parts) // 2
    for half in range(2):
        start = window_ref.shape[2]
        for ref in parts[half * count : (half + 1) * count]:
            size = ref.shape[1]
            mask = mask_ref[:, half_lanes(core, half, start, size)(gates)]
            gram += gram_sums(ref[...], mask, rows)
            pieces.append((half, start, ref))
            start += size
    weight_re, weight_im = solve(gram, steer_ref[...], bins_here, beams)

    def split(value):
        return [value[i : i + beams] for i in range(0, value.shape[0], beams)]

    for half, start, ref in pieces:
        for at in range(0, ref.shape[1], 128):
            lanes = half_lanes(core, half, start + at, 128)(gates)
            blocks = split(ref[:, at : at + 128])
            filter_gates(out_ref, lanes, blocks, weight_re, weight_im, beams)


def tail(me, steer, gram, window, mask, mine, theirs):
    bins_here, gates = mask.shape
    parts = mine + theirs
    return pl.pallas_call(
        tail_kernel,
        in_specs=[pl.BlockSpec(memory_space=pltpu.SMEM)]
        + [pl.BlockSpec(memory_space=pltpu.VMEM)] * (4 + len(parts)),
        out_shape=jax.ShapeDtypeStruct((bins_here, 2, gates), F32),
        compiler_params=pltpu.CompilerParams(vmem_limit_bytes=VMEM),
        cost_estimate=pl.CostEstimate(flops=1000, bytes_accessed=1000, transcendentals=0),
        name="tail",
    )(me, steer, gram, window, mask, *parts)


def slice_kernel(me_ref, echo_ref, part_ref):
    part_ref[...] = echo_ref[...]


def other_half(me, echo, start, size):
    elem_dev, rows_in, gate_count = echo.shape
    each = elem_dev // 2

    def lane(me):
        return pl.multiple_of((1 - me[0] % 2) * (gate_count // 2) + start, 128)

    return pl.pallas_call(
        slice_kernel,
        grid_spec=pltpu.PrefetchScalarGridSpec(
            num_scalar_prefetch=1,
            grid=(2,),
            in_specs=[
                pl.BlockSpec(
                    (pl.Element(each), pl.Element(rows_in), pl.Element(size)),
                    lambda i, me: (i * each, 0, lane(me)),
                )
            ],
            out_specs=pl.BlockSpec((each, rows_in, size), lambda i, me: (i, 0, 0)),
        ),
        out_shape=jax.ShapeDtypeStruct((elem_dev, rows_in, size), BF16),
        compiler_params=pltpu.CompilerParams(vmem_limit_bytes=VMEM),
        cost_estimate=pl.CostEstimate(flops=1000, bytes_accessed=1000, transcendentals=0),
        name="slice",
    )(me, echo)


def swap(x, stride, count):
    return lax.ppermute(x, "elem", [(i, i ^ stride) for i in range(count)])


def share_kernel(count, keep_ref, *refs):
    received, sends = refs[:count], refs[count:]
    total = keep_ref[...]
    for got in received:
        total = total + got[...].astype(F32)
    total = total.astype(BF16)
    tall = sends[0].shape[0]
    for i, out_ref in enumerate(reversed(sends)):
        out_ref[...] = total[i * tall : (i + 1) * tall]


def share(keep, received, height, parts):
    size = keep.shape[1]
    block = (height, size)
    second = pl.BlockSpec(block, lambda i: (1, 0))
    operands, specs = [keep], [second]
    for got in received[:-1]:
        operands.append(got[-1])
        specs.append(second)
    operands.append(received[-1][0])
    specs.append(second if len(received[-1]) == 1 else pl.BlockSpec(block, lambda i: (0, 0)))
    return pl.pallas_call(
        functools.partial(share_kernel, len(received)),
        grid=(1,),
        in_specs=specs,
        out_specs=[pl.BlockSpec((height // parts, size), lambda i: (0, 0))] * parts,
        out_shape=[jax.ShapeDtypeStruct((height // parts, size), BF16)] * parts,
        compiler_params=pltpu.CompilerParams(vmem_limit_bytes=VMEM),
        cost_estimate=pl.CostEstimate(flops=1000, bytes_accessed=1000, transcendentals=0),
        name="share",
    )(*operands)


def finish_kernel(step, me_ref, keep_ref, *refs):
    received, near_ref, send_ref, total_ref = refs[:-3], *refs[-3:]
    total = keep_ref[...]
    for got in received:
        total = total + got[...].astype(F32)
    total_ref[...] = total
    core = me_ref[0] % 2
    height = near_ref.shape[0]
    near_ref[...] = total_ref[pl.ds(pl.multiple_of(core * step, 8), height)]
    send_ref[...] = total_ref[pl.ds(pl.multiple_of((1 - core) * step, 8), height)]


def finish(me, keep, received, held, step):
    size = keep.shape[1]
    part = pl.BlockSpec((held, size), lambda i: (0, 0))
    out = pl.BlockSpec((held - step, size), lambda i: (0, 0))
    return pl.pallas_call(
        functools.partial(finish_kernel, step),
        grid=(1,),
        in_specs=[pl.BlockSpec(memory_space=pltpu.SMEM)] + [part] * (1 + len(received)),
        out_specs=[out, out],
        out_shape=[jax.ShapeDtypeStruct((held - step, size), F32)] * 2,
        scratch_shapes=[pltpu.VMEM((held, size), F32)],
        compiler_params=pltpu.CompilerParams(vmem_limit_bytes=VMEM),
        cost_estimate=pl.CostEstimate(flops=1000, bytes_accessed=1000, transcendentals=0),
        name="finish",
    )(me, keep, *received)


def edges_kernel(rows, step, me_ref, *refs):
    parts, out_ref = refs[:-1], refs[-1]
    first = pl.multiple_of(me_ref[0] % 2 * step, 8)
    start = 0
    for part in parts:
        size = part.shape[1]
        out_ref[:, start : start + size] = part[pl.ds(first, rows)]
        start += size


def edges(me, parts, rows):
    width = sum(x.shape[1] for x in parts)
    return pl.pallas_call(
        functools.partial(edges_kernel, rows, parts[0].shape[0] - rows),
        in_specs=[pl.BlockSpec(memory_space=pltpu.SMEM)]
        + [pl.BlockSpec(memory_space=pltpu.VMEM)] * len(parts),
        out_shape=jax.ShapeDtypeStruct((rows, width), F32),
        compiler_params=pltpu.CompilerParams(vmem_limit_bytes=VMEM),
        cost_estimate=pl.CostEstimate(flops=1000, bytes_accessed=1000, transcendentals=0),
        name="edges",
    )(me, *parts)


class Chain:
    def __init__(self):
        self.last = None

    def enter(self, value):
        if self.last is None:
            return value
        value, _ = lax.optimization_barrier((value, self.last))
        return value

    def leave(self, value):
        self.last = value
        return value


def local(raw_echo, beam_weights, steer, train_mask):
    elem_dev, _, pulses, gate_count = raw_echo.shape
    count = lax.axis_size("elem")
    me = lax.axis_index("elem").astype(jnp.int32)
    at = me.reshape(1)
    bins_here = pulses // count
    rows = 2 * beam_weights.shape[0]
    echo = raw_echo.reshape(elem_dev, 2 * pulses, gate_count)
    levels = count.bit_length() - 1
    plain = [2 << i for i in range(levels - 1)]
    orders = [plain, plain[1:] + plain[:1], [plain[1], plain[0]] + plain[2:]]
    unit = gate_count // 2 // sum(width for width, _, _, _ in CHUNKS)
    chunks = len(CHUNKS)
    last = sum(1 - wide for _, _, wide, _ in CHUNKS)
    spans = []
    for width, _, _, _ in CHUNKS:
        start = sum(spans[-1]) if spans else 0
        spans.append((start, width * unit))
    early = tuple(spans[:last])
    theirs = [None] * chunks
    keeps, received = [None] * chunks, [[] for _ in CHUNKS]
    near, far = [None] * chunks, [None] * chunks
    chain = Chain()
    edge = gram = window = None

    steps = []
    for c, stage in STEPS:
        if stage == 3:
            steps += [(c, later) for later in range(3, levels)]
        else:
            steps.append((c, levels if stage == 4 else stage))
    turns = [c for c, stage in steps if stage == 1]
    for c, stage in steps:
        if c == "halo":
            out = edges(at, far[:last] + near[:last], rows)
            pairs = [((i + 1) % count, i) for i in range(1, count, 2)]
            pairs += [(i, (i + 1) % count) for i in range(1, count, 2)]
            edge = lax.ppermute(out, "elem", pairs)
        elif c == "gram":
            gram, window = gram_of(at, early, near[:last], far[:last], edge, chain.enter(train_mask))
            chain.leave(gram)
        elif stage == 0:
            part = chain.leave(other_half(at, chain.enter(echo), *spans[c]))
            theirs[c] = swap(part, 1, count)
        elif stage >= 10:
            got = received[c][stage - 10]
            got[0] = chain.leave(chain.enter(got[0]))
        elif stage == 1:
            strides = orders[CHUNKS[c][1]]
            later = turns.index(c) + AHEAD
            later = turns[later] if later < chunks and (turns[later], 0) not in steps else None
            parts = 1 + CHUNKS[c][3]
            out = front(
                at, strides, CHUNKS[c][2], 2 * bins_here, beam_weights,
                chain.enter(echo), theirs[c], spans[c], None if later is None else spans[later], parts,
            )
            send, keeps[c], part = out[:parts], out[parts], out[parts + 1 :]
            if part:
                theirs[later] = swap(part[0], 1, count)
            chain.leave(send[0])
            received[c].append([swap(x, strides[0], count) for x in send])
        elif stage < levels:
            half = keeps[c].shape[0] >> (stage - 1)
            parts = 1 + CHUNKS[c][3] * (stage < levels - 1)
            send = share(chain.enter(keeps[c]), received[c], half, parts)
            chain.leave(send[0])
            received[c].append([swap(x, orders[CHUNKS[c][1]][stage - 1], count) for x in send])
        else:
            held = keeps[c].shape[0] >> (levels - 2)
            step = (bins_here - 1 + CHUNKS[c][2]) * rows
            near[c], send = finish(at, chain.enter(keeps[c]), [x[-1] for x in received[c]], held, step)
            chain.leave(send)
            far[c] = swap(send, 1, count)
    return tail(at, steer, gram, window, train_mask, near[last:], far[last:])


def solution(mesh):
    return jax.shard_map(
        local,
        mesh=mesh,
        in_specs=(P(("cpi", "elem"), None, None, None), P(), P(), P(("cpi", "elem"), None)),
        out_specs=P(("cpi", "elem"), None, None),
        check_vma=False,
    )
```

```python
import functools
import math

import jax
import jax.numpy as jnp
import ml_dtypes
import numpy as np
from jax import lax
from jax.experimental import pallas as pl
from jax.experimental.pallas import tpu as pltpu
from jax.sharding import PartitionSpec as P

LOADING = 1.0
F32 = jnp.float32
BF16 = jnp.bfloat16
GROUP = 8
VMEM = 48 << 20
CHUNKS = ((3, 0, 0, 0), (3, 0, 0, 0), (2, 1, 0, 0), (2, 0, 1, 0), (2, 0, 1, 1))
AHEAD = 2
STEPS = (
    (1, 0), (3, 0), (0, 0), (1, 1), (0, 1), (2, 1), (1, 2), (2, 2), (3, 1), (4, 1),
    (2, 3), (1, 3), (0, 2), (3, 2), (0, 11), (0, 3), (1, 4), (4, 2), (2, 4), (0, 4),
    (3, 3), ("halo", 0), (4, 3), (3, 4), ("gram", 0), (4, 4),
)


def block_at(strides):
    count = len(strides)
    blocks = []
    for position in range(1 << count):
        blocks.append(sum(s for i, s in enumerate(strides) if position >> (count - 1 - i) & 1))
    return blocks


def row_order(strides, bins_here, extra):
    rows = []
    for block in block_at(strides):
        for j in range(-extra, bins_here + extra):
            rows += [(block, 2 * j), (block, 2 * j + 1)]
    return np.array(rows, np.int32)


def doppler_table(pulses):
    index = np.arange(pulses)
    angles = (-2.0 * math.pi / pulses * (index[:, None] * index[None, :] % pulses)).astype(np.float32)
    cosine = np.cos(angles) / np.float32(math.sqrt(pulses))
    sine_part = np.sin(angles) / np.float32(math.sqrt(pulses))
    real_row = np.concatenate([cosine, -sine_part], axis=1)
    imag_row = np.concatenate([sine_part, cosine], axis=1)
    table = np.stack([real_row, imag_row], axis=1).reshape(2 * pulses, 2 * pulses)
    return table.astype(ml_dtypes.bfloat16)


def beam_picks(beams):
    picks = np.zeros((2, GROUP * 2 * beams, 2 * beams), np.float32)
    for g in range(GROUP):
        for b in range(beams):
            re_row, im_row = g * 2 * beams + b, g * 2 * beams + beams + b
            picks[0, re_row, b] = 1
            picks[0, im_row, beams + b] = 1
            picks[1, re_row, beams + b] = -1
            picks[1, im_row, b] = 1
    return picks.astype(ml_dtypes.bfloat16)


def dot(a, b):
    return jnp.dot(a, b, preferred_element_type=F32)


def front_kernel(
    bins_chip, ahead, parts, me_ref, order_ref, natural_ref, picks_ref, beam_ref, mine_ref, theirs_ref, *refs
):
    if ahead:
        refs[2 + parts][...] = refs[0][...]
        refs = refs[1 : 2 + parts] + refs[3 + parts :]
    sends, keep_ref, table_ref, weights_ref, spectra_ref = refs[:parts], *refs[parts:]
    elem_dev = mine_ref.shape[0]
    groups = spectra_ref.shape[0]
    width = mine_ref.shape[-1]
    rows_in = natural_ref.shape[0]
    me = me_ref[0]
    order = order_ref[...]
    source = jnp.bitwise_xor(order[:, 0:1], me // 2) * (2 * bins_chip) + order[:, 1:2]
    source = lax.rem(source + rows_in, rows_in)
    lane = lax.broadcasted_iota(jnp.int32, (order.shape[0], rows_in), 1)
    picked = jnp.where(source == lane, 1.0, 0.0).astype(BF16)
    table_ref[...] = dot(picked, natural_ref[...]).astype(BF16)
    given = beam_ref[...].astype(F32)
    given = jnp.concatenate([given[:, 0], given[:, 1]], axis=0).astype(BF16)
    elements = given.shape[1]
    columns = weights_ref.shape[1]
    row = lax.broadcasted_iota(jnp.int32, (elements, columns), 0)
    column = lax.broadcasted_iota(jnp.int32, (elements, columns), 1)
    held = column // (2 * GROUP)
    first = jnp.where(held < elem_dev, me, jnp.bitwise_xor(me, 1)) * elem_dev
    here = row == first + held % elem_dev
    total = jnp.zeros(weights_ref.shape, F32)
    for part in range(2):
        spread = jnp.where(here & (column % 2 == part), 1.0, 0.0).astype(BF16)
        total += dot(dot(picks_ref[part], given).astype(BF16), spread)
    row = lax.broadcasted_iota(jnp.int32, weights_ref.shape, 0)
    column = lax.broadcasted_iota(jnp.int32, weights_ref.shape, 1)
    same = row // (weights_ref.shape[0] // GROUP) == column % (2 * GROUP) // 2
    weights_ref[...] = jnp.where(same, total, 0.0).astype(BF16)

    table = table_ref[...]
    echoes = [mine_ref[e] for e in range(elem_dev)] + [theirs_ref[e] for e in range(elem_dev)]
    for e in range(0, 2 * elem_dev, 2):
        spectra = dot(table, jnp.concatenate(echoes[e : e + 2], axis=1)).astype(BF16)
        for i in range(2):
            part = spectra[:, i * width : (i + 1) * width]
            spectra_ref[:, e + i] = part.reshape(groups, 2 * GROUP, width)
    weights = weights_ref[...]
    rows = weights.shape[0]
    tall = sends[0].shape[0]
    for pair in range(0, groups, 2):
        spectra = [spectra_ref[g].reshape(-1, width) for g in (pair, pair + 1)]
        both = dot(weights, jnp.concatenate(spectra, axis=1))
        for g in (pair, pair + 1):
            sums = both[:, (g - pair) * width : (g - pair + 1) * width]
            if g < groups // 2:
                keep_ref[g * rows : (g + 1) * rows] = sums
                continue
            sums = sums.astype(BF16)
            for low in range(0, rows, 16):
                at = (g - groups // 2) * rows + low
                out_ref = sends[parts - 1 - at // tall]
                out_ref[at % tall : at % tall + 16] = sums[low : low + 16]


def front(me, strides, extra, bins_chip, beam_weights, echo, theirs, span, ahead, parts):
    elem_dev, rows_in, gate_count = echo.shape
    start, size = span
    beams = beam_weights.shape[0]
    order = row_order([s // 2 for s in strides], bins_chip, extra)
    natural = doppler_table(rows_in // 2)
    picks = beam_picks(beams)
    table_rows = order.shape[0]
    groups = table_rows // 2 // GROUP
    half = table_rows // 4 * 2 * beams
    block_rows, block_columns = GROUP * 2 * beams, elem_dev * 4 * GROUP
    whole = lambda shape: pl.BlockSpec(shape, lambda i, me: (0,) * len(shape))

    def gates(which, start, size):
        lane = lambda me: ((me[0] + which) % 2) * (gate_count // 2) + start
        return pl.BlockSpec(
            (pl.Element(elem_dev), pl.Element(rows_in), pl.Element(size)),
            lambda i, me: (0, 0, pl.multiple_of(lane(me), 128)),
        )

    in_specs = [whole(x.shape) for x in (order, natural, picks, beam_weights)]
    in_specs += [gates(0, start, size), whole(theirs.shape)]
    out_shape = [jax.ShapeDtypeStruct((half // parts, size), BF16)] * parts
    out_shape += [jax.ShapeDtypeStruct((half, size), F32)]
    operands = [me, jnp.asarray(order), jnp.asarray(natural), jnp.asarray(picks), beam_weights, echo, theirs]
    if ahead:
        in_specs.append(gates(1, *ahead))
        operands.append(echo)
        out_shape.append(jax.ShapeDtypeStruct((elem_dev, rows_in, ahead[1]), BF16))
    return pl.pallas_call(
        functools.partial(front_kernel, bins_chip, ahead is not None, parts),
        grid_spec=pltpu.PrefetchScalarGridSpec(
            num_scalar_prefetch=1,
            grid=(1,),
            in_specs=in_specs,
            out_specs=[whole(x.shape) for x in out_shape],
            scratch_shapes=[
                pltpu.VMEM((table_rows, rows_in), BF16),
                pltpu.VMEM((block_rows, block_columns), BF16),
                pltpu.VMEM((groups, 2 * elem_dev, 2 * GROUP, size), BF16),
            ],
        ),
        out_shape=out_shape,
        compiler_params=pltpu.CompilerParams(vmem_limit_bytes=VMEM),
        cost_estimate=pl.CostEstimate(flops=1000, bytes_accessed=1000, transcendentals=0),
        name="front",
    )(*operands)


def gram_sums(window, mask, rows):
    top = window.astype(BF16)
    rest = (window - top.astype(F32)).astype(BF16)
    picked_top, picked_rest = [], []
    for d in range(mask.shape[0]):
        keep = mask[d : d + 1].astype(F32).astype(BF16)
        picked_top.append(top[rows * d : rows * (d + 3)] * keep)
        picked_rest.append(rest[rows * d : rows * (d + 3)] * keep)
    left = jnp.concatenate(picked_top, axis=0)
    left_rest = jnp.concatenate(picked_rest, axis=0)
    dims = (((1,), (1,)), ((), ()))
    gram = lax.dot_general(left, top, dims, preferred_element_type=F32)
    gram += lax.dot_general(left, rest, dims, preferred_element_type=F32)
    gram += lax.dot_general(left_rest, top, dims, preferred_element_type=F32)
    return gram


def half_lanes(core, half, start, size):
    return lambda gates: pl.ds(pl.multiple_of((core ^ half) * (gates // 2) + start, 128), size)


def gram_kernel(spans, me_ref, edge_ref, mask_ref, *refs):
    parts, (gram_ref, window_ref) = refs[:-2], refs[-2:]
    rows = edge_ref.shape[0]
    inner = parts[0].shape[0]
    core = me_ref[0] % 2
    gates = mask_ref.shape[1]
    early = sum(size for _, size in spans)
    total = None
    for index, part in enumerate(parts):
        half, (start, size) = index // len(spans), spans[index % len(spans)]
        lanes = slice(start, start + size)
        inner_at = pl.multiple_of((1 - core) * rows, rows)
        edge_at = pl.multiple_of(core * inner, rows)
        window_ref[half, pl.ds(inner_at, inner), lanes] = part[...]
        edge = edge_ref[:, half * early + start : half * early + start + size]
        window_ref[half, pl.ds(edge_at, rows), lanes] = edge
        mask = mask_ref[:, half_lanes(core, half, start, size)(gates)]
        sums = gram_sums(window_ref[half, :, lanes], mask, rows)
        total = sums if total is None else total + sums
    gram_ref[...] = total


def gram_of(me, spans, mine, theirs, edge, mask):
    bins_here = mask.shape[0]
    rows = edge.shape[0]
    inner = mine[0].shape[0]
    early = sum(size for _, size in spans)
    return pl.pallas_call(
        functools.partial(gram_kernel, spans),
        in_specs=[pl.BlockSpec(memory_space=pltpu.SMEM)]
        + [pl.BlockSpec(memory_space=pltpu.VMEM)] * (2 + 2 * len(mine)),
        out_shape=[
            jax.ShapeDtypeStruct((bins_here * 3 * rows, inner + rows), F32),
            jax.ShapeDtypeStruct((2, inner + rows, early), F32),
        ],
        compiler_params=pltpu.CompilerParams(vmem_limit_bytes=VMEM),
        cost_estimate=pl.CostEstimate(flops=1000, bytes_accessed=1000, transcendentals=0),
        name="gram",
    )(me, edge, mask, *mine, *theirs)


def solve(gram, steer, bins_here, beams):
    rows, order = 2 * beams, 3 * beams
    lane = lax.broadcasted_iota(jnp.int32, (1, 1, 128), 2)
    real_lane = lane // beams % 2 == 0
    row_at = lax.broadcasted_iota(jnp.int32, (1, order, 128), 1)
    lane_at = lax.broadcasted_iota(jnp.int32, (1, order, 128), 2)
    diagonal = (lane_at // rows * beams + lane_at % beams == row_at) & (lane_at // beams % 2 == 0)
    diagonal &= lane_at < 3 * rows
    systems = []
    pad = jnp.zeros((3 * rows, 128 - 3 * rows), F32)
    for d in range(bins_here):
        block = gram[3 * rows * d : 3 * rows * (d + 1), rows * d : rows * (d + 3)]
        block = jnp.concatenate([block, pad], axis=1)
        pieces = [block[i : i + beams] for i in range(0, 3 * rows, beams)]
        from_re = jnp.concatenate(pieces[0::2], axis=0)
        from_im = jnp.concatenate(pieces[1::2], axis=0)
        real = from_re + pltpu.roll(from_im, 128 - beams, 1)
        imag = pltpu.roll(from_im, beams, 1) - from_re
        systems.append(jnp.where(real_lane[0], real, imag))
    system = jnp.stack(systems, axis=0)
    system = jnp.where(lane < 3 * rows, system, 0.0) + jnp.where(diagonal, LOADING, 0.0)
    pick = row_at[0, :, :order] == lane_at[0, :, :order]
    target_re = jnp.sum(jnp.where(pick, steer[0:1], 0.0), axis=1, keepdims=True)[None]
    target_im = jnp.sum(jnp.where(pick, steer[1:2], 0.0), axis=1, keepdims=True)[None]
    system = jnp.where(lane == 3 * rows, target_re, system)
    system = jnp.where(lane == 3 * rows + beams, target_im, system)

    def swapped(row):
        return jnp.where(real_lane[0], -pltpu.roll(row, 128 - beams, 1), pltpu.roll(row, beams, 1))

    across = jnp.transpose(system, (1, 0, 2))
    held = [across[i] for i in range(order)]
    for k in range(order):
        spot = k // beams * rows + k % beams
        pivot_row = held[k]
        turned = swapped(pivot_row)
        scale = 1.0 / jnp.broadcast_to(pivot_row[:, spot : spot + 1], pivot_row.shape)
        pivot_row, turned = pivot_row * scale, turned * scale
        for i in range(order):
            if i != k:
                factor_re = held[i][:, spot : spot + 1]
                factor_im = held[i][:, spot + beams : spot + beams + 1]
                held[i] = held[i] - factor_re * pivot_row - factor_im * turned
        held[k] = pivot_row

    solved_re = [row[:, 3 * rows : 3 * rows + 1] for row in held]
    solved_im = [row[:, 3 * rows + beams : 3 * rows + beams + 1] for row in held]
    response = jnp.zeros((bins_here, 1), F32)
    for i in range(order):
        response += solved_re[i] * target_re[0, i : i + 1] + solved_im[i] * target_im[0, i : i + 1]
    scale = 1.0 / jnp.broadcast_to(response, (bins_here, 128))
    weight_re = jnp.stack([part * scale for part in solved_re], axis=0)
    weight_im = jnp.stack([part * scale for part in solved_im], axis=0)
    return jnp.transpose(weight_re, (1, 0, 2)), jnp.transpose(weight_im, (1, 0, 2))


def filter_gates(out_ref, at, blocks, weight_re, weight_im, beams):
    for d in range(weight_re.shape[0]):
        total_re = jnp.zeros((beams, 128), F32)
        total_im = jnp.zeros((beams, 128), F32)
        for w in range(3):
            coeff_re = weight_re[d, w * beams : (w + 1) * beams]
            coeff_im = weight_im[d, w * beams : (w + 1) * beams]
            snap_re, snap_im = blocks[2 * (d + w)], blocks[2 * (d + w) + 1]
            total_re += coeff_re * snap_re + coeff_im * snap_im
            total_im += coeff_re * snap_im - coeff_im * snap_re
        row_re = jnp.sum(total_re, axis=0, keepdims=True)
        row_im = jnp.sum(total_im, axis=0, keepdims=True)
        out_ref[d, :, at] = jnp.concatenate([row_re, row_im], axis=0)


def tail_kernel(me_ref, steer_ref, gram_ref, window_ref, mask_ref, *refs):
    parts, out_ref = refs[:-1], refs[-1]
    bins_here, gates = mask_ref.shape
    rows = window_ref.shape[1] // (bins_here + 2)
    beams = rows // 2
    core = me_ref[0] % 2
    pieces = [(0, 0, window_ref.at[0]), (1, 0, window_ref.at[1])]
    gram = gram_ref[...]
    count = len(parts) // 2
    for half in range(2):
        start = window_ref.shape[2]
        for ref in parts[half * count : (half + 1) * count]:
            size = ref.shape[1]
            mask = mask_ref[:, half_lanes(core, half, start, size)(gates)]
            gram += gram_sums(ref[...], mask, rows)
            pieces.append((half, start, ref))
            start += size
    weight_re, weight_im = solve(gram, steer_ref[...], bins_here, beams)

    def split(value):
        return [value[i : i + beams] for i in range(0, value.shape[0], beams)]

    for half, start, ref in pieces:
        for at in range(0, ref.shape[1], 128):
            lanes = half_lanes(core, half, start + at, 128)(gates)
            blocks = split(ref[:, at : at + 128])
            filter_gates(out_ref, lanes, blocks, weight_re, weight_im, beams)


def tail(me, steer, gram, window, mask, mine, theirs):
    bins_here, gates = mask.shape
    parts = mine + theirs
    return pl.pallas_call(
        tail_kernel,
        in_specs=[pl.BlockSpec(memory_space=pltpu.SMEM)]
        + [pl.BlockSpec(memory_space=pltpu.VMEM)] * (4 + len(parts)),
        out_shape=jax.ShapeDtypeStruct((bins_here, 2, gates), F32),
        compiler_params=pltpu.CompilerParams(vmem_limit_bytes=VMEM),
        cost_estimate=pl.CostEstimate(flops=1000, bytes_accessed=1000, transcendentals=0),
        name="tail",
    )(me, steer, gram, window, mask, *parts)


def slice_kernel(me_ref, echo_ref, part_ref):
    part_ref[...] = echo_ref[...]


def other_half(me, echo, start, size):
    elem_dev, rows_in, gate_count = echo.shape
    each = elem_dev // 2

    def lane(me):
        return pl.multiple_of((1 - me[0] % 2) * (gate_count // 2) + start, 128)

    return pl.pallas_call(
        slice_kernel,
        grid_spec=pltpu.PrefetchScalarGridSpec(
            num_scalar_prefetch=1,
            grid=(2,),
            in_specs=[
                pl.BlockSpec(
                    (pl.Element(each), pl.Element(rows_in), pl.Element(size)),
                    lambda i, me: (i * each, 0, lane(me)),
                )
            ],
            out_specs=pl.BlockSpec((each, rows_in, size), lambda i, me: (i, 0, 0)),
        ),
        out_shape=jax.ShapeDtypeStruct((elem_dev, rows_in, size), BF16),
        compiler_params=pltpu.CompilerParams(vmem_limit_bytes=VMEM),
        cost_estimate=pl.CostEstimate(flops=1000, bytes_accessed=1000, transcendentals=0),
        name="slice",
    )(me, echo)


def swap(x, stride, count):
    return lax.ppermute(x, "elem", [(i, i ^ stride) for i in range(count)])


def share_kernel(count, keep_ref, *refs):
    received, sends = refs[:count], refs[count:]
    total = keep_ref[...]
    for got in received:
        total = total + got[...].astype(F32)
    total = total.astype(BF16)
    tall = sends[0].shape[0]
    for i, out_ref in enumerate(reversed(sends)):
        out_ref[...] = total[i * tall : (i + 1) * tall]


def share(keep, received, height, parts):
    size = keep.shape[1]
    block = (height, size)
    second = pl.BlockSpec(block, lambda i: (1, 0))
    operands, specs = [keep], [second]
    for got in received[:-1]:
        operands.append(got[-1])
        specs.append(second)
    operands.append(received[-1][0])
    specs.append(second if len(received[-1]) == 1 else pl.BlockSpec(block, lambda i: (0, 0)))
    return pl.pallas_call(
        functools.partial(share_kernel, len(received)),
        grid=(1,),
        in_specs=specs,
        out_specs=[pl.BlockSpec((height // parts, size), lambda i: (0, 0))] * parts,
        out_shape=[jax.ShapeDtypeStruct((height // parts, size), BF16)] * parts,
        compiler_params=pltpu.CompilerParams(vmem_limit_bytes=VMEM),
        cost_estimate=pl.CostEstimate(flops=1000, bytes_accessed=1000, transcendentals=0),
        name="share",
    )(*operands)


def finish_kernel(step, me_ref, keep_ref, *refs):
    received, near_ref, send_ref, total_ref = refs[:-3], *refs[-3:]
    total = keep_ref[...]
    for got in received:
        total = total + got[...].astype(F32)
    total_ref[...] = total
    core = me_ref[0] % 2
    height = near_ref.shape[0]
    near_ref[...] = total_ref[pl.ds(pl.multiple_of(core * step, 8), height)]
    send_ref[...] = total_ref[pl.ds(pl.multiple_of((1 - core) * step, 8), height)]


def finish(me, keep, received, held, step):
    size = keep.shape[1]
    part = pl.BlockSpec((held, size), lambda i: (0, 0))
    out = pl.BlockSpec((held - step, size), lambda i: (0, 0))
    return pl.pallas_call(
        functools.partial(finish_kernel, step),
        grid=(1,),
        in_specs=[pl.BlockSpec(memory_space=pltpu.SMEM)] + [part] * (1 + len(received)),
        out_specs=[out, out],
        out_shape=[jax.ShapeDtypeStruct((held - step, size), F32)] * 2,
        scratch_shapes=[pltpu.VMEM((held, size), F32)],
        compiler_params=pltpu.CompilerParams(vmem_limit_bytes=VMEM),
        cost_estimate=pl.CostEstimate(flops=1000, bytes_accessed=1000, transcendentals=0),
        name="finish",
    )(me, keep, *received)


def edges_kernel(rows, step, me_ref, *refs):
    parts, out_ref = refs[:-1], refs[-1]
    first = pl.multiple_of(me_ref[0] % 2 * step, 8)
    start = 0
    for part in parts:
        size = part.shape[1]
        out_ref[:, start : start + size] = part[pl.ds(first, rows)]
        start += size


def edges(me, parts, rows):
    width = sum(x.shape[1] for x in parts)
    return pl.pallas_call(
        functools.partial(edges_kernel, rows, parts[0].shape[0] - rows),
        in_specs=[pl.BlockSpec(memory_space=pltpu.SMEM)]
        + [pl.BlockSpec(memory_space=pltpu.VMEM)] * len(parts),
        out_shape=jax.ShapeDtypeStruct((rows, width), F32),
        compiler_params=pltpu.CompilerParams(vmem_limit_bytes=VMEM),
        cost_estimate=pl.CostEstimate(flops=1000, bytes_accessed=1000, transcendentals=0),
        name="edges",
    )(me, *parts)


class Chain:
    def __init__(self):
        self.last = None

    def enter(self, value):
        if self.last is None:
            return value
        value, _ = lax.optimization_barrier((value, self.last))
        return value

    def leave(self, value):
        self.last = value
        return value


def local(raw_echo, beam_weights, steer, train_mask):
    elem_dev, _, pulses, gate_count = raw_echo.shape
    count = lax.axis_size("elem")
    me = lax.axis_index("elem").astype(jnp.int32)
    at = me.reshape(1)
    bins_here = pulses // count
    rows = 2 * beam_weights.shape[0]
    echo = raw_echo.reshape(elem_dev, 2 * pulses, gate_count)
    levels = count.bit_length() - 1
    plain = [2 << i for i in range(levels - 1)]
    orders = [plain, plain[1:] + plain[:1], [plain[1], plain[0]] + plain[2:]]
    unit = gate_count // 2 // sum(width for width, _, _, _ in CHUNKS)
    chunks = len(CHUNKS)
    last = sum(1 - wide for _, _, wide, _ in CHUNKS)
    spans = []
    for width, _, _, _ in CHUNKS:
        start = sum(spans[-1]) if spans else 0
        spans.append((start, width * unit))
    early = tuple(spans[:last])
    theirs = [None] * chunks
    keeps, received = [None] * chunks, [[] for _ in CHUNKS]
    near, far = [None] * chunks, [None] * chunks
    chain = Chain()
    edge = gram = window = None

    steps = []
    for c, stage in STEPS:
        if stage == 3:
            steps += [(c, later) for later in range(3, levels)]
        else:
            steps.append((c, levels if stage == 4 else stage))
    turns = [c for c, stage in steps if stage == 1]
    for c, stage in steps:
        if c == "halo":
            out = edges(at, far[:last] + near[:last], rows)
            pairs = [((i + 1) % count, i) for i in range(1, count, 2)]
            pairs += [(i, (i + 1) % count) for i in range(1, count, 2)]
            edge = lax.ppermute(out, "elem", pairs)
        elif c == "gram":
            gram, window = gram_of(at, early, near[:last], far[:last], edge, chain.enter(train_mask))
            chain.leave(gram)
        elif stage == 0:
            part = chain.leave(other_half(at, chain.enter(echo), *spans[c]))
            theirs[c] = swap(part, 1, count)
        elif stage >= 10:
            got = received[c][stage - 10]
            got[0] = chain.leave(chain.enter(got[0]))
        elif stage == 1:
            strides = orders[CHUNKS[c][1]]
            later = turns.index(c) + AHEAD
            later = turns[later] if later < chunks and (turns[later], 0) not in steps else None
            parts = 1 + CHUNKS[c][3]
            out = front(
                at, strides, CHUNKS[c][2], 2 * bins_here, beam_weights,
                chain.enter(echo), theirs[c], spans[c], None if later is None else spans[later], parts,
            )
            send, keeps[c], part = out[:parts], out[parts], out[parts + 1 :]
            if part:
                theirs[later] = swap(part[0], 1, count)
            chain.leave(send[0])
            received[c].append([swap(x, strides[0], count) for x in send])
        elif stage < levels:
            half = keeps[c].shape[0] >> (stage - 1)
            parts = 1 + CHUNKS[c][3] * (stage < levels - 1)
            send = share(chain.enter(keeps[c]), received[c], half, parts)
            chain.leave(send[0])
            received[c].append([swap(x, orders[CHUNKS[c][1]][stage - 1], count) for x in send])
        else:
            held = keeps[c].shape[0] >> (levels - 2)
            step = (bins_here - 1 + CHUNKS[c][2]) * rows
            near[c], send = finish(at, chain.enter(keeps[c]), [x[-1] for x in received[c]], held, step)
            chain.leave(send)
            far[c] = swap(send, 1, count)
    return tail(at, steer, gram, window, train_mask, near[last:], far[last:])


def solution(mesh):
    return jax.shard_map(
        local,
        mesh=mesh,
        in_specs=(P(("cpi", "elem"), None, None, None), P(), P(), P(("cpi", "elem"), None)),
        out_specs=P(("cpi", "elem"), None, None),
        check_vma=False,
    )
```

```python
import functools
import math

import jax
import jax.numpy as jnp
import ml_dtypes
import numpy as np
from jax import lax
from jax.experimental import pallas as pl
from jax.experimental.pallas import tpu as pltpu
from jax.sharding import PartitionSpec as P

LOADING = 1.0
F32 = jnp.float32
BF16 = jnp.bfloat16
GROUP = 8
VMEM = 48 << 20
CHUNKS = ((3, 0, 0, 0), (3, 0, 0, 0), (2, 1, 0, 0), (2, 0, 1, 0), (2, 0, 1, 1))
AHEAD = 2
STEPS = (
    (1, 0), (3, 0), (0, 0), (1, 1), (0, 1), (2, 1), (1, 2), (2, 2), (3, 1), (4, 1),
    (2, 3), (1, 3), (0, 2), (3, 2), (0, 11), (0, 3), (1, 4), (4, 2), (2, 4), (0, 4),
    ("halo", 0), ("gram", 0), (3, 3), (4, 3), (3, 4), ("edge", 0), (4, 4),
)


def block_at(strides):
    count = len(strides)
    blocks = []
    for position in range(1 << count):
        blocks.append(sum(s for i, s in enumerate(strides) if position >> (count - 1 - i) & 1))
    return blocks


def row_order(strides, bins_here, extra):
    rows = []
    for block in block_at(strides):
        for j in range(-extra, bins_here + extra):
            rows += [(block, 2 * j), (block, 2 * j + 1)]
    return np.array(rows, np.int32)


def doppler_table(pulses):
    index = np.arange(pulses)
    angles = (-2.0 * math.pi / pulses * (index[:, None] * index[None, :] % pulses)).astype(np.float32)
    cosine = np.cos(angles) / np.float32(math.sqrt(pulses))
    sine_part = np.sin(angles) / np.float32(math.sqrt(pulses))
    real_row = np.concatenate([cosine, -sine_part], axis=1)
    imag_row = np.concatenate([sine_part, cosine], axis=1)
    table = np.stack([real_row, imag_row], axis=1).reshape(2 * pulses, 2 * pulses)
    return table.astype(ml_dtypes.bfloat16)


def beam_picks(beams):
    picks = np.zeros((2, GROUP * 2 * beams, 2 * beams), np.float32)
    for g in range(GROUP):
        for b in range(beams):
            re_row, im_row = g * 2 * beams + b, g * 2 * beams + beams + b
            picks[0, re_row, b] = 1
            picks[0, im_row, beams + b] = 1
            picks[1, re_row, beams + b] = -1
            picks[1, im_row, b] = 1
    return picks.astype(ml_dtypes.bfloat16)


def dot(a, b):
    return jnp.dot(a, b, preferred_element_type=F32)


def front_kernel(
    bins_chip, ahead, parts, me_ref, order_ref, natural_ref, picks_ref, beam_ref, mine_ref, theirs_ref, *refs
):
    if ahead:
        refs[2 + parts][...] = refs[0][...]
        refs = refs[1 : 2 + parts] + refs[3 + parts :]
    sends, keep_ref, table_ref, weights_ref, spectra_ref = refs[:parts], *refs[parts:]
    elem_dev = mine_ref.shape[0]
    groups = spectra_ref.shape[0]
    width = mine_ref.shape[-1]
    rows_in = natural_ref.shape[0]
    me = me_ref[0]
    order = order_ref[...]
    source = jnp.bitwise_xor(order[:, 0:1], me // 2) * (2 * bins_chip) + order[:, 1:2]
    source = lax.rem(source + rows_in, rows_in)
    lane = lax.broadcasted_iota(jnp.int32, (order.shape[0], rows_in), 1)
    picked = jnp.where(source == lane, 1.0, 0.0).astype(BF16)
    table_ref[...] = dot(picked, natural_ref[...]).astype(BF16)
    given = beam_ref[...].astype(F32)
    given = jnp.concatenate([given[:, 0], given[:, 1]], axis=0).astype(BF16)
    elements = given.shape[1]
    columns = weights_ref.shape[1]
    row = lax.broadcasted_iota(jnp.int32, (elements, columns), 0)
    column = lax.broadcasted_iota(jnp.int32, (elements, columns), 1)
    held = column // (2 * GROUP)
    first = jnp.where(held < elem_dev, me, jnp.bitwise_xor(me, 1)) * elem_dev
    here = row == first + held % elem_dev
    total = jnp.zeros(weights_ref.shape, F32)
    for part in range(2):
        spread = jnp.where(here & (column % 2 == part), 1.0, 0.0).astype(BF16)
        total += dot(dot(picks_ref[part], given).astype(BF16), spread)
    row = lax.broadcasted_iota(jnp.int32, weights_ref.shape, 0)
    column = lax.broadcasted_iota(jnp.int32, weights_ref.shape, 1)
    same = row // (weights_ref.shape[0] // GROUP) == column % (2 * GROUP) // 2
    weights_ref[...] = jnp.where(same, total, 0.0).astype(BF16)

    table = table_ref[...]
    echoes = [mine_ref[e] for e in range(elem_dev)] + [theirs_ref[e] for e in range(elem_dev)]
    for e in range(0, 2 * elem_dev, 2):
        spectra = dot(table, jnp.concatenate(echoes[e : e + 2], axis=1)).astype(BF16)
        for i in range(2):
            part = spectra[:, i * width : (i + 1) * width]
            spectra_ref[:, e + i] = part.reshape(groups, 2 * GROUP, width)
    weights = weights_ref[...]
    rows = weights.shape[0]
    tall = sends[0].shape[0]
    for pair in range(0, groups, 2):
        spectra = [spectra_ref[g].reshape(-1, width) for g in (pair, pair + 1)]
        both = dot(weights, jnp.concatenate(spectra, axis=1))
        for g in (pair, pair + 1):
            sums = both[:, (g - pair) * width : (g - pair + 1) * width]
            if g < groups // 2:
                keep_ref[g * rows : (g + 1) * rows] = sums
                continue
            sums = sums.astype(BF16)
            for low in range(0, rows, 16):
                at = (g - groups // 2) * rows + low
                out_ref = sends[parts - 1 - at // tall]
                out_ref[at % tall : at % tall + 16] = sums[low : low + 16]


def front(me, strides, extra, bins_chip, beam_weights, echo, theirs, span, ahead, parts):
    elem_dev, rows_in, gate_count = echo.shape
    start, size = span
    beams = beam_weights.shape[0]
    order = row_order([s // 2 for s in strides], bins_chip, extra)
    natural = doppler_table(rows_in // 2)
    picks = beam_picks(beams)
    table_rows = order.shape[0]
    groups = table_rows // 2 // GROUP
    half = table_rows // 4 * 2 * beams
    block_rows, block_columns = GROUP * 2 * beams, elem_dev * 4 * GROUP
    whole = lambda shape: pl.BlockSpec(shape, lambda i, me: (0,) * len(shape))

    def gates(which, start, size):
        lane = lambda me: ((me[0] + which) % 2) * (gate_count // 2) + start
        return pl.BlockSpec(
            (pl.Element(elem_dev), pl.Element(rows_in), pl.Element(size)),
            lambda i, me: (0, 0, pl.multiple_of(lane(me), 128)),
        )

    in_specs = [whole(x.shape) for x in (order, natural, picks, beam_weights)]
    in_specs += [gates(0, start, size), whole(theirs.shape)]
    out_shape = [jax.ShapeDtypeStruct((half // parts, size), BF16)] * parts
    out_shape += [jax.ShapeDtypeStruct((half, size), F32)]
    operands = [me, jnp.asarray(order), jnp.asarray(natural), jnp.asarray(picks), beam_weights, echo, theirs]
    if ahead:
        in_specs.append(gates(1, *ahead))
        operands.append(echo)
        out_shape.append(jax.ShapeDtypeStruct((elem_dev, rows_in, ahead[1]), BF16))
    return pl.pallas_call(
        functools.partial(front_kernel, bins_chip, ahead is not None, parts),
        grid_spec=pltpu.PrefetchScalarGridSpec(
            num_scalar_prefetch=1,
            grid=(1,),
            in_specs=in_specs,
            out_specs=[whole(x.shape) for x in out_shape],
            scratch_shapes=[
                pltpu.VMEM((table_rows, rows_in), BF16),
                pltpu.VMEM((block_rows, block_columns), BF16),
                pltpu.VMEM((groups, 2 * elem_dev, 2 * GROUP, size), BF16),
            ],
        ),
        out_shape=out_shape,
        compiler_params=pltpu.CompilerParams(vmem_limit_bytes=VMEM),
        cost_estimate=pl.CostEstimate(flops=1000, bytes_accessed=1000, transcendentals=0),
        name="front",
    )(*operands)


def gram_sums(window, mask, rows):
    top = window.astype(BF16)
    rest = (window - top.astype(F32)).astype(BF16)
    picked_top, picked_rest = [], []
    for d in range(mask.shape[0]):
        keep = mask[d : d + 1].astype(F32).astype(BF16)
        picked_top.append(top[rows * d : rows * (d + 3)] * keep)
        picked_rest.append(rest[rows * d : rows * (d + 3)] * keep)
    left = jnp.concatenate(picked_top, axis=0)
    left_rest = jnp.concatenate(picked_rest, axis=0)
    dims = (((1,), (1,)), ((), ()))
    gram = lax.dot_general(left, top, dims, preferred_element_type=F32)
    gram += lax.dot_general(left, rest, dims, preferred_element_type=F32)
    gram += lax.dot_general(left_rest, top, dims, preferred_element_type=F32)
    return gram


def half_lanes(core, half, start, size):
    return lambda gates: pl.ds(pl.multiple_of((core ^ half) * (gates // 2) + start, 128), size)


def gram_kernel(spans, rows, me_ref, mask_ref, *refs):
    parts, (gram_ref, window_ref) = refs[:-2], refs[-2:]
    inner = parts[0].shape[0]
    core = me_ref[0] % 2
    gates = mask_ref.shape[1]
    total = None
    for index, part in enumerate(parts):
        half, (start, size) = index // len(spans), spans[index % len(spans)]
        lanes = slice(start, start + size)
        inner_at = pl.multiple_of((1 - core) * rows, rows)
        edge_at = pl.multiple_of(core * inner, rows)
        window_ref[half, pl.ds(inner_at, inner), lanes] = part[...]
        window_ref[half, pl.ds(edge_at, rows), lanes] = jnp.zeros((rows, size), F32)
        mask = mask_ref[:, half_lanes(core, half, start, size)(gates)]
        sums = gram_sums(window_ref[half, :, lanes], mask, rows)
        total = sums if total is None else total + sums
    gram_ref[...] = total


def gram_of(me, spans, mine, theirs, mask, rows):
    bins_here = mask.shape[0]
    inner = mine[0].shape[0]
    early = sum(size for _, size in spans)
    return pl.pallas_call(
        functools.partial(gram_kernel, spans, rows),
        in_specs=[pl.BlockSpec(memory_space=pltpu.SMEM)]
        + [pl.BlockSpec(memory_space=pltpu.VMEM)] * (1 + 2 * len(mine)),
        out_shape=[
            jax.ShapeDtypeStruct((bins_here * 3 * rows, inner + rows), F32),
            jax.ShapeDtypeStruct((2, inner + rows, early), F32),
        ],
        compiler_params=pltpu.CompilerParams(vmem_limit_bytes=VMEM),
        cost_estimate=pl.CostEstimate(flops=1000, bytes_accessed=1000, transcendentals=0),
        name="gram",
    )(me, mask, *mine, *theirs)


def split_dot(left, right, mask):
    dims = (((1,), (1,)), ((), ()))
    keep = mask.astype(BF16)
    tops = [x.astype(BF16) for x in (left, right)]
    rests = [(x - top.astype(F32)).astype(BF16) for x, top in zip((left, right), tops)]
    total = lax.dot_general(tops[0] * keep, tops[1], dims, preferred_element_type=F32)
    total += lax.dot_general(tops[0] * keep, rests[1], dims, preferred_element_type=F32)
    return total + lax.dot_general(rests[0] * keep, tops[1], dims, preferred_element_type=F32)


def edge_sums(core, edge, window, mask, rows):
    last = window.shape[0] - 3 * rows
    held = jnp.where(core == 0, window[: 3 * rows], window[last:])
    held = jnp.concatenate(
        [
            jnp.where(core == 0, edge, held[:rows]),
            held[rows : 2 * rows],
            jnp.where(core == 0, held[2 * rows :], edge),
        ],
        axis=0,
    )
    mask = jnp.where(core == 0, mask[0:1], mask[mask.shape[0] - 1 :]).astype(F32)
    columns = split_dot(held, edge, mask)
    lane = lax.broadcasted_iota(jnp.int32, (rows, 3 * rows), 1)
    first = core * 2 * rows
    others = (lane < first) | (lane >= first + rows)
    across = jnp.where(others, split_dot(edge, held, mask), 0.0)
    blank = jnp.zeros((3 * rows, 2 * rows), F32)
    columns = jnp.where(
        core == 0,
        jnp.concatenate([columns, blank], axis=1),
        jnp.concatenate([blank, columns], axis=1),
    )
    blank = jnp.zeros((2 * rows, 3 * rows), F32)
    across = jnp.where(
        core == 0,
        jnp.concatenate([across, blank], axis=0),
        jnp.concatenate([blank, across], axis=0),
    )
    return columns + across


def solve(gram, extra, core, steer, bins_here, beams):
    rows, order = 2 * beams, 3 * beams
    lane = lax.broadcasted_iota(jnp.int32, (1, 1, 128), 2)
    real_lane = lane // beams % 2 == 0
    row_at = lax.broadcasted_iota(jnp.int32, (1, order, 128), 1)
    lane_at = lax.broadcasted_iota(jnp.int32, (1, order, 128), 2)
    diagonal = (lane_at // rows * beams + lane_at % beams == row_at) & (lane_at // beams % 2 == 0)
    diagonal &= lane_at < 3 * rows
    systems = []
    pad = jnp.zeros((3 * rows, 128 - 3 * rows), F32)
    for d in range(bins_here):
        block = gram[3 * rows * d : 3 * rows * (d + 1), rows * d : rows * (d + 3)]
        if d == 0:
            block = block + jnp.where(core == 0, extra, 0.0)
        if d == bins_here - 1:
            block = block + jnp.where(core == 1, extra, 0.0)
        block = jnp.concatenate([block, pad], axis=1)
        pieces = [block[i : i + beams] for i in range(0, 3 * rows, beams)]
        from_re = jnp.concatenate(pieces[0::2], axis=0)
        from_im = jnp.concatenate(pieces[1::2], axis=0)
        real = from_re + pltpu.roll(from_im, 128 - beams, 1)
        imag = pltpu.roll(from_im, beams, 1) - from_re
        systems.append(jnp.where(real_lane[0], real, imag))
    system = jnp.stack(systems, axis=0)
    system = jnp.where(lane < 3 * rows, system, 0.0) + jnp.where(diagonal, LOADING, 0.0)
    pick = row_at[0, :, :order] == lane_at[0, :, :order]
    target_re = jnp.sum(jnp.where(pick, steer[0:1], 0.0), axis=1, keepdims=True)[None]
    target_im = jnp.sum(jnp.where(pick, steer[1:2], 0.0), axis=1, keepdims=True)[None]
    system = jnp.where(lane == 3 * rows, target_re, system)
    system = jnp.where(lane == 3 * rows + beams, target_im, system)

    def swapped(row):
        return jnp.where(real_lane[0], -pltpu.roll(row, 128 - beams, 1), pltpu.roll(row, beams, 1))

    across = jnp.transpose(system, (1, 0, 2))
    held = [across[i] for i in range(order)]
    for k in range(order):
        spot = k // beams * rows + k % beams
        pivot_row = held[k]
        turned = swapped(pivot_row)
        scale = 1.0 / jnp.broadcast_to(pivot_row[:, spot : spot + 1], pivot_row.shape)
        pivot_row, turned = pivot_row * scale, turned * scale
        for i in range(order):
            if i != k:
                factor_re = held[i][:, spot : spot + 1]
                factor_im = held[i][:, spot + beams : spot + beams + 1]
                held[i] = held[i] - factor_re * pivot_row - factor_im * turned
        held[k] = pivot_row

    solved_re = [row[:, 3 * rows : 3 * rows + 1] for row in held]
    solved_im = [row[:, 3 * rows + beams : 3 * rows + beams + 1] for row in held]
    response = jnp.zeros((bins_here, 1), F32)
    for i in range(order):
        response += solved_re[i] * target_re[0, i : i + 1] + solved_im[i] * target_im[0, i : i + 1]
    scale = 1.0 / jnp.broadcast_to(response, (bins_here, 128))
    weight_re = jnp.stack([part * scale for part in solved_re], axis=0)
    weight_im = jnp.stack([part * scale for part in solved_im], axis=0)
    return jnp.transpose(weight_re, (1, 0, 2)), jnp.transpose(weight_im, (1, 0, 2))


def filter_gates(out_ref, at, blocks, weight_re, weight_im, beams):
    for d in range(weight_re.shape[0]):
        total_re = jnp.zeros((beams, 128), F32)
        total_im = jnp.zeros((beams, 128), F32)
        for w in range(3):
            coeff_re = weight_re[d, w * beams : (w + 1) * beams]
            coeff_im = weight_im[d, w * beams : (w + 1) * beams]
            snap_re, snap_im = blocks[2 * (d + w)], blocks[2 * (d + w) + 1]
            total_re += coeff_re * snap_re + coeff_im * snap_im
            total_im += coeff_re * snap_im - coeff_im * snap_re
        row_re = jnp.sum(total_re, axis=0, keepdims=True)
        row_im = jnp.sum(total_im, axis=0, keepdims=True)
        out_ref[d, :, at] = jnp.concatenate([row_re, row_im], axis=0)


def tail_kernel(me_ref, steer_ref, gram_ref, window_ref, edge_ref, mask_ref, *refs):
    parts, out_ref = refs[:-1], refs[-1]
    bins_here, gates = mask_ref.shape
    rows = window_ref.shape[1] // (bins_here + 2)
    beams = rows // 2
    core = me_ref[0] % 2
    early = window_ref.shape[2]
    edge = edge_ref[...]
    early_mask = [mask_ref[:, half_lanes(core, half, 0, early)(gates)] for half in range(2)]
    early_window = jnp.concatenate([window_ref[0], window_ref[1]], axis=1)
    extra = edge_sums(core, edge, early_window, jnp.concatenate(early_mask, axis=1), rows)
    pieces = [(0, 0, window_ref.at[0]), (1, 0, window_ref.at[1])]
    gram = gram_ref[...]
    count = len(parts) // 2
    for half in range(2):
        start = window_ref.shape[2]
        for ref in parts[half * count : (half + 1) * count]:
            size = ref.shape[1]
            mask = mask_ref[:, half_lanes(core, half, start, size)(gates)]
            gram += gram_sums(ref[...], mask, rows)
            pieces.append((half, start, ref))
            start += size
    weight_re, weight_im = solve(gram, extra, core, steer_ref[...], bins_here, beams)

    def split(value):
        return [value[i : i + beams] for i in range(0, value.shape[0], beams)]

    for half, start, ref in pieces:
        for at in range(0, ref.shape[1], 128):
            lanes = half_lanes(core, half, start + at, 128)(gates)
            value = ref[:, at : at + 128]
            blocks = split(value)
            if start == 0:
                part = edge[:, half * early + at : half * early + at + 128]
                low, high = value[:rows], value[value.shape[0] - rows :]
                blocks[:2] = split(jnp.where(core == 0, part, low))
                blocks[-2:] = split(jnp.where(core == 0, high, part))
            filter_gates(out_ref, lanes, blocks, weight_re, weight_im, beams)


def tail(me, steer, gram, window, edge, mask, mine, theirs):
    bins_here, gates = mask.shape
    parts = mine + theirs
    return pl.pallas_call(
        tail_kernel,
        in_specs=[pl.BlockSpec(memory_space=pltpu.SMEM)]
        + [pl.BlockSpec(memory_space=pltpu.VMEM)] * (5 + len(parts)),
        out_shape=jax.ShapeDtypeStruct((bins_here, 2, gates), F32),
        compiler_params=pltpu.CompilerParams(vmem_limit_bytes=VMEM),
        cost_estimate=pl.CostEstimate(flops=1000, bytes_accessed=1000, transcendentals=0),
        name="tail",
    )(me, steer, gram, window, edge, mask, *parts)


def slice_kernel(me_ref, echo_ref, part_ref):
    part_ref[...] = echo_ref[...]


def other_half(me, echo, start, size):
    elem_dev, rows_in, gate_count = echo.shape
    each = elem_dev // 2

    def lane(me):
        return pl.multiple_of((1 - me[0] % 2) * (gate_count // 2) + start, 128)

    return pl.pallas_call(
        slice_kernel,
        grid_spec=pltpu.PrefetchScalarGridSpec(
            num_scalar_prefetch=1,
            grid=(2,),
            in_specs=[
                pl.BlockSpec(
                    (pl.Element(each), pl.Element(rows_in), pl.Element(size)),
                    lambda i, me: (i * each, 0, lane(me)),
                )
            ],
            out_specs=pl.BlockSpec((each, rows_in, size), lambda i, me: (i, 0, 0)),
        ),
        out_shape=jax.ShapeDtypeStruct((elem_dev, rows_in, size), BF16),
        compiler_params=pltpu.CompilerParams(vmem_limit_bytes=VMEM),
        cost_estimate=pl.CostEstimate(flops=1000, bytes_accessed=1000, transcendentals=0),
        name="slice",
    )(me, echo)


def swap(x, stride, count):
    return lax.ppermute(x, "elem", [(i, i ^ stride) for i in range(count)])


def share_kernel(count, keep_ref, *refs):
    received, sends = refs[:count], refs[count:]
    total = keep_ref[...]
    for got in received:
        total = total + got[...].astype(F32)
    total = total.astype(BF16)
    tall = sends[0].shape[0]
    for i, out_ref in enumerate(reversed(sends)):
        out_ref[...] = total[i * tall : (i + 1) * tall]


def share(keep, received, height, parts):
    size = keep.shape[1]
    block = (height, size)
    second = pl.BlockSpec(block, lambda i: (1, 0))
    operands, specs = [keep], [second]
    for got in received[:-1]:
        operands.append(got[-1])
        specs.append(second)
    operands.append(received[-1][0])
    specs.append(second if len(received[-1]) == 1 else pl.BlockSpec(block, lambda i: (0, 0)))
    return pl.pallas_call(
        functools.partial(share_kernel, len(received)),
        grid=(1,),
        in_specs=specs,
        out_specs=[pl.BlockSpec((height // parts, size), lambda i: (0, 0))] * parts,
        out_shape=[jax.ShapeDtypeStruct((height // parts, size), BF16)] * parts,
        compiler_params=pltpu.CompilerParams(vmem_limit_bytes=VMEM),
        cost_estimate=pl.CostEstimate(flops=1000, bytes_accessed=1000, transcendentals=0),
        name="share",
    )(*operands)


def finish_kernel(step, me_ref, keep_ref, *refs):
    received, near_ref, send_ref, total_ref = refs[:-3], *refs[-3:]
    total = keep_ref[...]
    for got in received:
        total = total + got[...].astype(F32)
    total_ref[...] = total
    core = me_ref[0] % 2
    height = near_ref.shape[0]
    near_ref[...] = total_ref[pl.ds(pl.multiple_of(core * step, 8), height)]
    send_ref[...] = total_ref[pl.ds(pl.multiple_of((1 - core) * step, 8), height)]


def finish(me, keep, received, held, step):
    size = keep.shape[1]
    part = pl.BlockSpec((held, size), lambda i: (0, 0))
    out = pl.BlockSpec((held - step, size), lambda i: (0, 0))
    return pl.pallas_call(
        functools.partial(finish_kernel, step),
        grid=(1,),
        in_specs=[pl.BlockSpec(memory_space=pltpu.SMEM)] + [part] * (1 + len(received)),
        out_specs=[out, out],
        out_shape=[jax.ShapeDtypeStruct((held - step, size), F32)] * 2,
        scratch_shapes=[pltpu.VMEM((held, size), F32)],
        compiler_params=pltpu.CompilerParams(vmem_limit_bytes=VMEM),
        cost_estimate=pl.CostEstimate(flops=1000, bytes_accessed=1000, transcendentals=0),
        name="finish",
    )(me, keep, *received)


def edges_kernel(rows, step, me_ref, *refs):
    parts, out_ref = refs[:-1], refs[-1]
    first = pl.multiple_of(me_ref[0] % 2 * step, 8)
    start = 0
    for part in parts:
        size = part.shape[1]
        out_ref[:, start : start + size] = part[pl.ds(first, rows)]
        start += size


def edges(me, parts, rows):
    width = sum(x.shape[1] for x in parts)
    return pl.pallas_call(
        functools.partial(edges_kernel, rows, parts[0].shape[0] - rows),
        in_specs=[pl.BlockSpec(memory_space=pltpu.SMEM)]
        + [pl.BlockSpec(memory_space=pltpu.VMEM)] * len(parts),
        out_shape=jax.ShapeDtypeStruct((rows, width), F32),
        compiler_params=pltpu.CompilerParams(vmem_limit_bytes=VMEM),
        cost_estimate=pl.CostEstimate(flops=1000, bytes_accessed=1000, transcendentals=0),
        name="edges",
    )(me, *parts)


class Chain:
    def __init__(self):
        self.last = None

    def enter(self, value):
        if self.last is None:
            return value
        value, _ = lax.optimization_barrier((value, self.last))
        return value

    def leave(self, value):
        self.last = value
        return value


def local(raw_echo, beam_weights, steer, train_mask):
    elem_dev, _, pulses, gate_count = raw_echo.shape
    count = lax.axis_size("elem")
    me = lax.axis_index("elem").astype(jnp.int32)
    at = me.reshape(1)
    bins_here = pulses // count
    rows = 2 * beam_weights.shape[0]
    echo = raw_echo.reshape(elem_dev, 2 * pulses, gate_count)
    levels = count.bit_length() - 1
    plain = [2 << i for i in range(levels - 1)]
    orders = [plain, plain[1:] + plain[:1], [plain[1], plain[0]] + plain[2:]]
    unit = gate_count // 2 // sum(width for width, _, _, _ in CHUNKS)
    chunks = len(CHUNKS)
    last = sum(1 - wide for _, _, wide, _ in CHUNKS)
    spans = []
    for width, _, _, _ in CHUNKS:
        start = sum(spans[-1]) if spans else 0
        spans.append((start, width * unit))
    early = tuple(spans[:last])
    theirs = [None] * chunks
    keeps, received = [None] * chunks, [[] for _ in CHUNKS]
    near, far = [None] * chunks, [None] * chunks
    chain = Chain()
    edge = gram = window = None

    steps = []
    for c, stage in STEPS:
        if stage == 3:
            steps += [(c, later) for later in range(3, levels)]
        else:
            steps.append((c, levels if stage == 4 else stage))
    turns = [c for c, stage in steps if stage == 1]
    for c, stage in steps:
        if c == "halo":
            out = edges(at, far[:last] + near[:last], rows)
            pairs = [((i + 1) % count, i) for i in range(1, count, 2)]
            pairs += [(i, (i + 1) % count) for i in range(1, count, 2)]
            edge = lax.ppermute(out, "elem", pairs)
        elif c == "gram":
            mask = chain.enter(train_mask)
            gram, window = gram_of(at, early, near[:last], far[:last], mask, rows)
            chain.leave(gram)
        elif c == "edge":
            edge = chain.leave(chain.enter(edge))
        elif stage == 0:
            part = chain.leave(other_half(at, chain.enter(echo), *spans[c]))
            theirs[c] = swap(part, 1, count)
        elif stage >= 10:
            got = received[c][stage - 10]
            got[0] = chain.leave(chain.enter(got[0]))
        elif stage == 1:
            strides = orders[CHUNKS[c][1]]
            later = turns.index(c) + AHEAD
            later = turns[later] if later < chunks and (turns[later], 0) not in steps else None
            parts = 1 + CHUNKS[c][3]
            out = front(
                at, strides, CHUNKS[c][2], 2 * bins_here, beam_weights,
                chain.enter(echo), theirs[c], spans[c], None if later is None else spans[later], parts,
            )
            send, keeps[c], part = out[:parts], out[parts], out[parts + 1 :]
            if part:
                theirs[later] = swap(part[0], 1, count)
            chain.leave(send[0])
            received[c].append([swap(x, strides[0], count) for x in send])
        elif stage < levels:
            half = keeps[c].shape[0] >> (stage - 1)
            parts = 1 + CHUNKS[c][3] * (stage < levels - 1)
            send = share(chain.enter(keeps[c]), received[c], half, parts)
            chain.leave(send[0])
            received[c].append([swap(x, orders[CHUNKS[c][1]][stage - 1], count) for x in send])
        else:
            held = keeps[c].shape[0] >> (levels - 2)
            step = (bins_here - 1 + CHUNKS[c][2]) * rows
            near[c], send = finish(at, chain.enter(keeps[c]), [x[-1] for x in received[c]], held, step)
            chain.leave(send)
            far[c] = swap(send, 1, count)
    return tail(at, steer, gram, window, edge, train_mask, near[last:], far[last:])


def solution(mesh):
    return jax.shard_map(
        local,
        mesh=mesh,
        in_specs=(P(("cpi", "elem"), None, None, None), P(), P(), P(("cpi", "elem"), None)),
        out_specs=P(("cpi", "elem"), None, None),
        check_vma=False,
    )
```

```python
import functools
import math

import jax
import jax.numpy as jnp
import ml_dtypes
import numpy as np
from jax import lax
from jax.experimental import pallas as pl
from jax.experimental.pallas import tpu as pltpu
from jax.sharding import PartitionSpec as P

LOADING = 1.0
F32 = jnp.float32
BF16 = jnp.bfloat16
GROUP = 8
VMEM = 48 << 20
CHUNKS = ((3, 0, 0, 0), (3, 0, 0, 0), (2, 1, 0, 0), (2, 0, 1, 0), (2, 0, 1, 1))
AHEAD = 2
STEPS = (
    (1, 0), (3, 0), (0, 0), (1, 1), (0, 1), (2, 1), (1, 2), (2, 2), (3, 1), (4, 1),
    (2, 3), (1, 3), (0, 2), (3, 2), (0, 11), (0, 3), (1, 4), (4, 2), (2, 4), (0, 4),
    ("halo", 0), ("gram", 0), (3, 3), (4, 3), (3, 4), ("edge", 0), (4, 4),
)


def block_at(strides):
    count = len(strides)
    blocks = []
    for position in range(1 << count):
        blocks.append(sum(s for i, s in enumerate(strides) if position >> (count - 1 - i) & 1))
    return blocks


def row_order(strides, bins_here, extra):
    rows = []
    for block in block_at(strides):
        for j in range(-extra, bins_here + extra):
            rows += [(block, 2 * j), (block, 2 * j + 1)]
    return np.array(rows, np.int32)


def doppler_table(pulses):
    index = np.arange(pulses)
    angles = (-2.0 * math.pi / pulses * (index[:, None] * index[None, :] % pulses)).astype(np.float32)
    cosine = np.cos(angles) / np.float32(math.sqrt(pulses))
    sine_part = np.sin(angles) / np.float32(math.sqrt(pulses))
    real_row = np.concatenate([cosine, -sine_part], axis=1)
    imag_row = np.concatenate([sine_part, cosine], axis=1)
    table = np.stack([real_row, imag_row], axis=1).reshape(2 * pulses, 2 * pulses)
    return table.astype(ml_dtypes.bfloat16)


def beam_picks(beams):
    picks = np.zeros((2, GROUP * 2 * beams, 2 * beams), np.float32)
    for g in range(GROUP):
        for b in range(beams):
            re_row, im_row = g * 2 * beams + b, g * 2 * beams + beams + b
            picks[0, re_row, b] = 1
            picks[0, im_row, beams + b] = 1
            picks[1, re_row, beams + b] = -1
            picks[1, im_row, b] = 1
    return picks.astype(ml_dtypes.bfloat16)


def dot(a, b):
    return jnp.dot(a, b, preferred_element_type=F32)


def front_kernel(
    bins_chip, ahead, parts, me_ref, order_ref, natural_ref, picks_ref, beam_ref, mine_ref, theirs_ref, *refs
):
    if ahead:
        refs[2 + parts][...] = refs[0][...]
        refs = refs[1 : 2 + parts] + refs[3 + parts :]
    sends, keep_ref, table_ref, weights_ref, spectra_ref = refs[:parts], *refs[parts:]
    each = mine_ref.shape[0]
    elem_dev = 2 * each
    groups = spectra_ref.shape[0]
    width = mine_ref.shape[-1]
    rows_in = natural_ref.shape[0]
    step = pl.program_id(0)

    @pl.when(step == 0)
    def _():
        me = me_ref[0]
        order = order_ref[...]
        source = jnp.bitwise_xor(order[:, 0:1], me // 2) * (2 * bins_chip) + order[:, 1:2]
        source = lax.rem(source + rows_in, rows_in)
        lane = lax.broadcasted_iota(jnp.int32, (order.shape[0], rows_in), 1)
        picked = jnp.where(source == lane, 1.0, 0.0).astype(BF16)
        table_ref[...] = dot(picked, natural_ref[...]).astype(BF16)
        given = beam_ref[...].astype(F32)
        given = jnp.concatenate([given[:, 0], given[:, 1]], axis=0).astype(BF16)
        elements = given.shape[1]
        columns = weights_ref.shape[1]
        row = lax.broadcasted_iota(jnp.int32, (elements, columns), 0)
        column = lax.broadcasted_iota(jnp.int32, (elements, columns), 1)
        held = column // (2 * GROUP)
        first = jnp.where(held < elem_dev, me, jnp.bitwise_xor(me, 1)) * elem_dev
        here = row == first + held % elem_dev
        total = jnp.zeros(weights_ref.shape, F32)
        for part in range(2):
            spread = jnp.where(here & (column % 2 == part), 1.0, 0.0).astype(BF16)
            total += dot(dot(picks_ref[part], given).astype(BF16), spread)
        row = lax.broadcasted_iota(jnp.int32, weights_ref.shape, 0)
        column = lax.broadcasted_iota(jnp.int32, weights_ref.shape, 1)
        same = row // (weights_ref.shape[0] // GROUP) == column % (2 * GROUP) // 2
        weights_ref[...] = jnp.where(same, total, 0.0).astype(BF16)

    table = table_ref[...]
    for held, echo_ref in ((0, mine_ref), (elem_dev, theirs_ref)):
        for j in range(0, each, 2):
            spectra = dot(table, jnp.concatenate([echo_ref[j], echo_ref[j + 1]], axis=1)).astype(BF16)
            for i in range(2):
                part = spectra[:, i * width : (i + 1) * width]
                spectra_ref[:, held + step * each + j + i] = part.reshape(groups, 2 * GROUP, width)

    @pl.when(step == 1)
    def _():
        weights = weights_ref[...]
        rows = weights.shape[0]
        tall = sends[0].shape[0]
        for pair in range(0, groups, 2):
            spectra = [spectra_ref[g].reshape(-1, width) for g in (pair, pair + 1)]
            both = dot(weights, jnp.concatenate(spectra, axis=1))
            for g in (pair, pair + 1):
                sums = both[:, (g - pair) * width : (g - pair + 1) * width]
                if g < groups // 2:
                    keep_ref[g * rows : (g + 1) * rows] = sums
                    continue
                sums = sums.astype(BF16)
                for low in range(0, rows, 16):
                    at = (g - groups // 2) * rows + low
                    out_ref = sends[parts - 1 - at // tall]
                    out_ref[at % tall : at % tall + 16] = sums[low : low + 16]


def front(me, strides, extra, bins_chip, beam_weights, echo, theirs, span, ahead, parts):
    elem_dev, rows_in, gate_count = echo.shape
    start, size = span
    beams = beam_weights.shape[0]
    order = row_order([s // 2 for s in strides], bins_chip, extra)
    natural = doppler_table(rows_in // 2)
    picks = beam_picks(beams)
    table_rows = order.shape[0]
    groups = table_rows // 2 // GROUP
    half = table_rows // 4 * 2 * beams
    block_rows, block_columns = GROUP * 2 * beams, elem_dev * 4 * GROUP
    whole = lambda shape: pl.BlockSpec(shape, lambda i, me: (0,) * len(shape))

    each = elem_dev // 2

    def gates(which, start, size):
        lane = lambda me: ((me[0] + which) % 2) * (gate_count // 2) + start
        return pl.BlockSpec(
            (pl.Element(each), pl.Element(rows_in), pl.Element(size)),
            lambda i, me: (i * each, 0, pl.multiple_of(lane(me), 128)),
        )

    in_specs = [whole(x.shape) for x in (order, natural, picks, beam_weights)]
    in_specs += [
        gates(0, start, size),
        pl.BlockSpec((each, rows_in, size), lambda i, me: (i, 0, 0)),
    ]
    out_shape = [jax.ShapeDtypeStruct((half // parts, size), BF16)] * parts
    out_shape += [jax.ShapeDtypeStruct((half, size), F32)]
    out_specs = [whole(x.shape) for x in out_shape]
    operands = [me, jnp.asarray(order), jnp.asarray(natural), jnp.asarray(picks), beam_weights, echo, theirs]
    if ahead:
        in_specs.append(gates(1, *ahead))
        operands.append(echo)
        out_shape.append(jax.ShapeDtypeStruct((elem_dev, rows_in, ahead[1]), BF16))
        out_specs.append(pl.BlockSpec((each, rows_in, ahead[1]), lambda i, me: (i, 0, 0)))
    return pl.pallas_call(
        functools.partial(front_kernel, bins_chip, ahead is not None, parts),
        grid_spec=pltpu.PrefetchScalarGridSpec(
            num_scalar_prefetch=1,
            grid=(2,),
            in_specs=in_specs,
            out_specs=out_specs,
            scratch_shapes=[
                pltpu.VMEM((table_rows, rows_in), BF16),
                pltpu.VMEM((block_rows, block_columns), BF16),
                pltpu.VMEM((groups, 2 * elem_dev, 2 * GROUP, size), BF16),
            ],
        ),
        out_shape=out_shape,
        compiler_params=pltpu.CompilerParams(vmem_limit_bytes=VMEM),
        cost_estimate=pl.CostEstimate(flops=1000, bytes_accessed=1000, transcendentals=0),
        name="front",
    )(*operands)


def gram_sums(window, mask, rows):
    top = window.astype(BF16)
    rest = (window - top.astype(F32)).astype(BF16)
    picked_top, picked_rest = [], []
    for d in range(mask.shape[0]):
        keep = mask[d : d + 1].astype(F32).astype(BF16)
        picked_top.append(top[rows * d : rows * (d + 3)] * keep)
        picked_rest.append(rest[rows * d : rows * (d + 3)] * keep)
    left = jnp.concatenate(picked_top, axis=0)
    left_rest = jnp.concatenate(picked_rest, axis=0)
    dims = (((1,), (1,)), ((), ()))
    gram = lax.dot_general(left, top, dims, preferred_element_type=F32)
    gram += lax.dot_general(left, rest, dims, preferred_element_type=F32)
    gram += lax.dot_general(left_rest, top, dims, preferred_element_type=F32)
    return gram


def half_lanes(core, half, start, size):
    return lambda gates: pl.ds(pl.multiple_of((core ^ half) * (gates // 2) + start, 128), size)


def gram_kernel(spans, rows, me_ref, mask_ref, *refs):
    parts, (gram_ref, window_ref) = refs[:-2], refs[-2:]
    inner = parts[0].shape[0]
    core = me_ref[0] % 2
    gates = mask_ref.shape[1]
    total = None
    for index, part in enumerate(parts):
        half, (start, size) = index // len(spans), spans[index % len(spans)]
        lanes = slice(start, start + size)
        inner_at = pl.multiple_of((1 - core) * rows, rows)
        edge_at = pl.multiple_of(core * inner, rows)
        window_ref[half, pl.ds(inner_at, inner), lanes] = part[...]
        window_ref[half, pl.ds(edge_at, rows), lanes] = jnp.zeros((rows, size), F32)
        mask = mask_ref[:, half_lanes(core, half, start, size)(gates)]
        sums = gram_sums(window_ref[half, :, lanes], mask, rows)
        total = sums if total is None else total + sums
    gram_ref[...] = total


def gram_of(me, spans, mine, theirs, mask, rows):
    bins_here = mask.shape[0]
    inner = mine[0].shape[0]
    early = sum(size for _, size in spans)
    return pl.pallas_call(
        functools.partial(gram_kernel, spans, rows),
        in_specs=[pl.BlockSpec(memory_space=pltpu.SMEM)]
        + [pl.BlockSpec(memory_space=pltpu.VMEM)] * (1 + 2 * len(mine)),
        out_shape=[
            jax.ShapeDtypeStruct((bins_here * 3 * rows, inner + rows), F32),
            jax.ShapeDtypeStruct((2, inner + rows, early), F32),
        ],
        compiler_params=pltpu.CompilerParams(vmem_limit_bytes=VMEM),
        cost_estimate=pl.CostEstimate(flops=1000, bytes_accessed=1000, transcendentals=0),
        name="gram",
    )(me, mask, *mine, *theirs)


def split_dot(left, right, mask):
    dims = (((1,), (1,)), ((), ()))
    keep = mask.astype(BF16)
    tops = [x.astype(BF16) for x in (left, right)]
    rests = [(x - top.astype(F32)).astype(BF16) for x, top in zip((left, right), tops)]
    total = lax.dot_general(tops[0] * keep, tops[1], dims, preferred_element_type=F32)
    total += lax.dot_general(tops[0] * keep, rests[1], dims, preferred_element_type=F32)
    return total + lax.dot_general(rests[0] * keep, tops[1], dims, preferred_element_type=F32)


def edge_sums(core, edge, window, mask, rows):
    last = window.shape[0] - 3 * rows
    held = jnp.where(core == 0, window[: 3 * rows], window[last:])
    held = jnp.concatenate(
        [
            jnp.where(core == 0, edge, held[:rows]),
            held[rows : 2 * rows],
            jnp.where(core == 0, held[2 * rows :], edge),
        ],
        axis=0,
    )
    mask = jnp.where(core == 0, mask[0:1], mask[mask.shape[0] - 1 :]).astype(F32)
    columns = split_dot(held, edge, mask)
    lane = lax.broadcasted_iota(jnp.int32, (rows, 3 * rows), 1)
    first = core * 2 * rows
    others = (lane < first) | (lane >= first + rows)
    across = jnp.where(others, split_dot(edge, held, mask), 0.0)
    blank = jnp.zeros((3 * rows, 2 * rows), F32)
    columns = jnp.where(
        core == 0,
        jnp.concatenate([columns, blank], axis=1),
        jnp.concatenate([blank, columns], axis=1),
    )
    blank = jnp.zeros((2 * rows, 3 * rows), F32)
    across = jnp.where(
        core == 0,
        jnp.concatenate([across, blank], axis=0),
        jnp.concatenate([blank, across], axis=0),
    )
    return columns + across


def solve(gram, extra, core, steer, bins_here, beams):
    rows, order = 2 * beams, 3 * beams
    lane = lax.broadcasted_iota(jnp.int32, (1, 1, 128), 2)
    real_lane = lane // beams % 2 == 0
    row_at = lax.broadcasted_iota(jnp.int32, (1, order, 128), 1)
    lane_at = lax.broadcasted_iota(jnp.int32, (1, order, 128), 2)
    diagonal = (lane_at // rows * beams + lane_at % beams == row_at) & (lane_at // beams % 2 == 0)
    diagonal &= lane_at < 3 * rows
    systems = []
    pad = jnp.zeros((3 * rows, 128 - 3 * rows), F32)
    for d in range(bins_here):
        block = gram[3 * rows * d : 3 * rows * (d + 1), rows * d : rows * (d + 3)]
        if d == 0:
            block = block + jnp.where(core == 0, extra, 0.0)
        if d == bins_here - 1:
            block = block + jnp.where(core == 1, extra, 0.0)
        block = jnp.concatenate([block, pad], axis=1)
        pieces = [block[i : i + beams] for i in range(0, 3 * rows, beams)]
        from_re = jnp.concatenate(pieces[0::2], axis=0)
        from_im = jnp.concatenate(pieces[1::2], axis=0)
        real = from_re + pltpu.roll(from_im, 128 - beams, 1)
        imag = pltpu.roll(from_im, beams, 1) - from_re
        systems.append(jnp.where(real_lane[0], real, imag))
    system = jnp.stack(systems, axis=0)
    system = jnp.where(lane < 3 * rows, system, 0.0) + jnp.where(diagonal, LOADING, 0.0)
    pick = row_at[0, :, :order] == lane_at[0, :, :order]
    target_re = jnp.sum(jnp.where(pick, steer[0:1], 0.0), axis=1, keepdims=True)[None]
    target_im = jnp.sum(jnp.where(pick, steer[1:2], 0.0), axis=1, keepdims=True)[None]
    system = jnp.where(lane == 3 * rows, target_re, system)
    system = jnp.where(lane == 3 * rows + beams, target_im, system)

    def swapped(row):
        return jnp.where(real_lane[0], -pltpu.roll(row, 128 - beams, 1), pltpu.roll(row, beams, 1))

    across = jnp.transpose(system, (1, 0, 2))
    held = [across[i] for i in range(order)]
    for k in range(order):
        spot = k // beams * rows + k % beams
        pivot_row = held[k]
        turned = swapped(pivot_row)
        scale = 1.0 / jnp.broadcast_to(pivot_row[:, spot : spot + 1], pivot_row.shape)
        pivot_row, turned = pivot_row * scale, turned * scale
        for i in range(order):
            if i != k:
                factor_re = held[i][:, spot : spot + 1]
                factor_im = held[i][:, spot + beams : spot + beams + 1]
                held[i] = held[i] - factor_re * pivot_row - factor_im * turned
        held[k] = pivot_row

    solved_re = [row[:, 3 * rows : 3 * rows + 1] for row in held]
    solved_im = [row[:, 3 * rows + beams : 3 * rows + beams + 1] for row in held]
    response = jnp.zeros((bins_here, 1), F32)
    for i in range(order):
        response += solved_re[i] * target_re[0, i : i + 1] + solved_im[i] * target_im[0, i : i + 1]
    scale = 1.0 / jnp.broadcast_to(response, (bins_here, 128))
    weight_re = jnp.stack([part * scale for part in solved_re], axis=0)
    weight_im = jnp.stack([part * scale for part in solved_im], axis=0)
    return jnp.transpose(weight_re, (1, 0, 2)), jnp.transpose(weight_im, (1, 0, 2))


def filter_gates(out_ref, at, blocks, weight_re, weight_im, beams):
    for d in range(weight_re.shape[0]):
        total_re = jnp.zeros((beams, 128), F32)
        total_im = jnp.zeros((beams, 128), F32)
        for w in range(3):
            coeff_re = weight_re[d, w * beams : (w + 1) * beams]
            coeff_im = weight_im[d, w * beams : (w + 1) * beams]
            snap_re, snap_im = blocks[2 * (d + w)], blocks[2 * (d + w) + 1]
            total_re += coeff_re * snap_re + coeff_im * snap_im
            total_im += coeff_re * snap_im - coeff_im * snap_re
        row_re = jnp.sum(total_re, axis=0, keepdims=True)
        row_im = jnp.sum(total_im, axis=0, keepdims=True)
        out_ref[d, :, at] = jnp.concatenate([row_re, row_im], axis=0)


def tail_kernel(me_ref, steer_ref, gram_ref, window_ref, edge_ref, mask_ref, *refs):
    parts, out_ref = refs[:-1], refs[-1]
    bins_here, gates = mask_ref.shape
    rows = window_ref.shape[1] // (bins_here + 2)
    beams = rows // 2
    core = me_ref[0] % 2
    early = window_ref.shape[2]
    edge = edge_ref[...]
    early_mask = [mask_ref[:, half_lanes(core, half, 0, early)(gates)] for half in range(2)]
    early_window = jnp.concatenate([window_ref[0], window_ref[1]], axis=1)
    extra = edge_sums(core, edge, early_window, jnp.concatenate(early_mask, axis=1), rows)
    pieces = [(0, 0, window_ref.at[0]), (1, 0, window_ref.at[1])]
    gram = gram_ref[...]
    count = len(parts) // 2
    for half in range(2):
        start = window_ref.shape[2]
        for ref in parts[half * count : (half + 1) * count]:
            size = ref.shape[1]
            mask = mask_ref[:, half_lanes(core, half, start, size)(gates)]
            gram += gram_sums(ref[...], mask, rows)
            pieces.append((half, start, ref))
            start += size
    weight_re, weight_im = solve(gram, extra, core, steer_ref[...], bins_here, beams)

    def split(value):
        return [value[i : i + beams] for i in range(0, value.shape[0], beams)]

    for half, start, ref in pieces:
        for at in range(0, ref.shape[1], 128):
            lanes = half_lanes(core, half, start + at, 128)(gates)
            value = ref[:, at : at + 128]
            blocks = split(value)
            if start == 0:
                part = edge[:, half * early + at : half * early + at + 128]
                low, high = value[:rows], value[value.shape[0] - rows :]
                blocks[:2] = split(jnp.where(core == 0, part, low))
                blocks[-2:] = split(jnp.where(core == 0, high, part))
            filter_gates(out_ref, lanes, blocks, weight_re, weight_im, beams)


def tail(me, steer, gram, window, edge, mask, mine, theirs):
    bins_here, gates = mask.shape
    parts = mine + theirs
    return pl.pallas_call(
        tail_kernel,
        in_specs=[pl.BlockSpec(memory_space=pltpu.SMEM)]
        + [pl.BlockSpec(memory_space=pltpu.VMEM)] * (5 + len(parts)),
        out_shape=jax.ShapeDtypeStruct((bins_here, 2, gates), F32),
        compiler_params=pltpu.CompilerParams(vmem_limit_bytes=VMEM),
        cost_estimate=pl.CostEstimate(flops=1000, bytes_accessed=1000, transcendentals=0),
        name="tail",
    )(me, steer, gram, window, edge, mask, *parts)


def slice_kernel(me_ref, echo_ref, part_ref):
    part_ref[...] = echo_ref[...]


def other_half(me, echo, start, size):
    elem_dev, rows_in, gate_count = echo.shape
    each = elem_dev // 2

    def lane(me):
        return pl.multiple_of((1 - me[0] % 2) * (gate_count // 2) + start, 128)

    return pl.pallas_call(
        slice_kernel,
        grid_spec=pltpu.PrefetchScalarGridSpec(
            num_scalar_prefetch=1,
            grid=(2,),
            in_specs=[
                pl.BlockSpec(
                    (pl.Element(each), pl.Element(rows_in), pl.Element(size)),
                    lambda i, me: (i * each, 0, lane(me)),
                )
            ],
            out_specs=pl.BlockSpec((each, rows_in, size), lambda i, me: (i, 0, 0)),
        ),
        out_shape=jax.ShapeDtypeStruct((elem_dev, rows_in, size), BF16),
        compiler_params=pltpu.CompilerParams(vmem_limit_bytes=VMEM),
        cost_estimate=pl.CostEstimate(flops=1000, bytes_accessed=1000, transcendentals=0),
        name="slice",
    )(me, echo)


def swap(x, stride, count):
    return lax.ppermute(x, "elem", [(i, i ^ stride) for i in range(count)])


def share_kernel(count, keep_ref, *refs):
    received, sends = refs[:count], refs[count:]
    total = keep_ref[...]
    for got in received:
        total = total + got[...].astype(F32)
    total = total.astype(BF16)
    tall = sends[0].shape[0]
    for i, out_ref in enumerate(reversed(sends)):
        out_ref[...] = total[i * tall : (i + 1) * tall]


def share(keep, received, height, parts):
    size = keep.shape[1]
    block = (height, size)
    second = pl.BlockSpec(block, lambda i: (1, 0))
    operands, specs = [keep], [second]
    for got in received[:-1]:
        operands.append(got[-1])
        specs.append(second)
    operands.append(received[-1][0])
    specs.append(second if len(received[-1]) == 1 else pl.BlockSpec(block, lambda i: (0, 0)))
    return pl.pallas_call(
        functools.partial(share_kernel, len(received)),
        grid=(1,),
        in_specs=specs,
        out_specs=[pl.BlockSpec((height // parts, size), lambda i: (0, 0))] * parts,
        out_shape=[jax.ShapeDtypeStruct((height // parts, size), BF16)] * parts,
        compiler_params=pltpu.CompilerParams(vmem_limit_bytes=VMEM),
        cost_estimate=pl.CostEstimate(flops=1000, bytes_accessed=1000, transcendentals=0),
        name="share",
    )(*operands)


def finish_kernel(step, me_ref, keep_ref, *refs):
    received, near_ref, send_ref, total_ref = refs[:-3], *refs[-3:]
    total = keep_ref[...]
    for got in received:
        total = total + got[...].astype(F32)
    total_ref[...] = total
    core = me_ref[0] % 2
    height = near_ref.shape[0]
    near_ref[...] = total_ref[pl.ds(pl.multiple_of(core * step, 8), height)]
    send_ref[...] = total_ref[pl.ds(pl.multiple_of((1 - core) * step, 8), height)]


def finish(me, keep, received, held, step):
    size = keep.shape[1]
    part = pl.BlockSpec((held, size), lambda i: (0, 0))
    out = pl.BlockSpec((held - step, size), lambda i: (0, 0))
    return pl.pallas_call(
        functools.partial(finish_kernel, step),
        grid=(1,),
        in_specs=[pl.BlockSpec(memory_space=pltpu.SMEM)] + [part] * (1 + len(received)),
        out_specs=[out, out],
        out_shape=[jax.ShapeDtypeStruct((held - step, size), F32)] * 2,
        scratch_shapes=[pltpu.VMEM((held, size), F32)],
        compiler_params=pltpu.CompilerParams(vmem_limit_bytes=VMEM),
        cost_estimate=pl.CostEstimate(flops=1000, bytes_accessed=1000, transcendentals=0),
        name="finish",
    )(me, keep, *received)


def edges_kernel(rows, step, me_ref, *refs):
    parts, out_ref = refs[:-1], refs[-1]
    first = pl.multiple_of(me_ref[0] % 2 * step, 8)
    start = 0
    for part in parts:
        size = part.shape[1]
        out_ref[:, start : start + size] = part[pl.ds(first, rows)]
        start += size


def edges(me, parts, rows):
    width = sum(x.shape[1] for x in parts)
    return pl.pallas_call(
        functools.partial(edges_kernel, rows, parts[0].shape[0] - rows),
        in_specs=[pl.BlockSpec(memory_space=pltpu.SMEM)]
        + [pl.BlockSpec(memory_space=pltpu.VMEM)] * len(parts),
        out_shape=jax.ShapeDtypeStruct((rows, width), F32),
        compiler_params=pltpu.CompilerParams(vmem_limit_bytes=VMEM),
        cost_estimate=pl.CostEstimate(flops=1000, bytes_accessed=1000, transcendentals=0),
        name="edges",
    )(me, *parts)


class Chain:
    def __init__(self):
        self.last = None

    def enter(self, value):
        if self.last is None:
            return value
        value, _ = lax.optimization_barrier((value, self.last))
        return value

    def leave(self, value):
        self.last = value
        return value


def local(raw_echo, beam_weights, steer, train_mask):
    elem_dev, _, pulses, gate_count = raw_echo.shape
    count = lax.axis_size("elem")
    me = lax.axis_index("elem").astype(jnp.int32)
    at = me.reshape(1)
    bins_here = pulses // count
    rows = 2 * beam_weights.shape[0]
    echo = raw_echo.reshape(elem_dev, 2 * pulses, gate_count)
    levels = count.bit_length() - 1
    plain = [2 << i for i in range(levels - 1)]
    orders = [plain, plain[1:] + plain[:1], [plain[1], plain[0]] + plain[2:]]
    unit = gate_count // 2 // sum(width for width, _, _, _ in CHUNKS)
    chunks = len(CHUNKS)
    last = sum(1 - wide for _, _, wide, _ in CHUNKS)
    spans = []
    for width, _, _, _ in CHUNKS:
        start = sum(spans[-1]) if spans else 0
        spans.append((start, width * unit))
    early = tuple(spans[:last])
    theirs = [None] * chunks
    keeps, received = [None] * chunks, [[] for _ in CHUNKS]
    near, far = [None] * chunks, [None] * chunks
    chain = Chain()
    edge = gram = window = None

    steps = []
    for c, stage in STEPS:
        if stage == 3:
            steps += [(c, later) for later in range(3, levels)]
        else:
            steps.append((c, levels if stage == 4 else stage))
    turns = [c for c, stage in steps if stage == 1]
    for c, stage in steps:
        if c == "halo":
            out = edges(at, far[:last] + near[:last], rows)
            pairs = [((i + 1) % count, i) for i in range(1, count, 2)]
            pairs += [(i, (i + 1) % count) for i in range(1, count, 2)]
            edge = lax.ppermute(out, "elem", pairs)
        elif c == "gram":
            mask = chain.enter(train_mask)
            gram, window = gram_of(at, early, near[:last], far[:last], mask, rows)
            chain.leave(gram)
        elif c == "edge":
            edge = chain.leave(chain.enter(edge))
        elif stage == 0:
            part = chain.leave(other_half(at, chain.enter(echo), *spans[c]))
            theirs[c] = swap(part, 1, count)
        elif stage >= 10:
            got = received[c][stage - 10]
            got[0] = chain.leave(chain.enter(got[0]))
        elif stage == 1:
            strides = orders[CHUNKS[c][1]]
            later = turns.index(c) + AHEAD
            later = turns[later] if later < chunks and (turns[later], 0) not in steps else None
            parts = 1 + CHUNKS[c][3]
            out = front(
                at, strides, CHUNKS[c][2], 2 * bins_here, beam_weights,
                chain.enter(echo), theirs[c], spans[c], None if later is None else spans[later], parts,
            )
            send, keeps[c], part = out[:parts], out[parts], out[parts + 1 :]
            if part:
                theirs[later] = swap(part[0], 1, count)
            chain.leave(send[0])
            received[c].append([swap(x, strides[0], count) for x in send])
        elif stage < levels:
            half = keeps[c].shape[0] >> (stage - 1)
            parts = 1 + CHUNKS[c][3] * (stage < levels - 1)
            send = share(chain.enter(keeps[c]), received[c], half, parts)
            chain.leave(send[0])
            received[c].append([swap(x, orders[CHUNKS[c][1]][stage - 1], count) for x in send])
        else:
            held = keeps[c].shape[0] >> (levels - 2)
            step = (bins_here - 1 + CHUNKS[c][2]) * rows
            near[c], send = finish(at, chain.enter(keeps[c]), [x[-1] for x in received[c]], held, step)
            chain.leave(send)
            far[c] = swap(send, 1, count)
    return tail(at, steer, gram, window, edge, train_mask, near[last:], far[last:])


def solution(mesh):
    return jax.shard_map(
        local,
        mesh=mesh,
        in_specs=(P(("cpi", "elem"), None, None, None), P(), P(), P(("cpi", "elem"), None)),
        out_specs=P(("cpi", "elem"), None, None),
        check_vma=False,
    )
```
